32 devices in a mesh: loop: 4 (over x, core), groups: 8 (over z, y).
Axes of the slice: x: 2, y: 2, z: 4, core: 2. Of those that a mesh axis runs over, the one named last changes fastest.
Arguments:
- states: bfloat16 [4096, 1024], P(('loop', 'groups')), may hold values from -64 to 64
- premises: bfloat16 [4096, 1024], P(('loop', 'groups')), may hold values from -1 to 1
- counts: int32 [4, 8], P('loop', 'groups'), may hold values from 64 to 128, as said below
- partner_mask: int32 [4], P('loop'), may hold values from 0 to 7, as said below
- send_rows: int32 [4, 8, 16], P('loop', 'groups'), may hold values from 0 to 63
- hard_idx: int32 [4096], P(('loop', 'groups')), may hold values from 0 to 15
Outputs:
- loss: float32 [], replicated
- grad_states: bfloat16 [4096, 1024], P(('loop', 'groups'))
- grad_premises: bfloat16 [4096, 1024], P(('loop', 'groups'))
The draws below stay inside these ranges and needn't reach their ends.
Inputs may be any that keep to these rules, and one draw needn't show every extreme that they name: `counts`: at least 64 valid pairs on every device; some device has all slots valid. `partner_mask`: loop index 0 has the value 8 // 2.
All inputs are finite; a program needn't handle non-finite values.
Results may differ from the reference program's by a relative error of at most 0.0034.
Values may be sent and summed in bfloat16 or wider, within the bound.
No kernel may reach another device: no remote copies, remote signals or barrier semaphores. Data moves between devices by JAX's collectives and lax.ppermute only.
A program may use at most 64 MiB of HBM per device.

```python
import jax
import jax.numpy as jnp
from jax import lax

D = 1024
TOK_DEV = 128
HARD = 16
PAIRS = 4096
N_LOOP = 4
N_GROUPS = 8


def pair_fields(key):
    key_a, key_b = jax.random.split(jax.random.fold_in(key, 11))
    prem = jnp.clip(jax.random.normal(key_a, (PAIRS, D), jnp.float32), -6.0, 6.0) * D ** (-0.5)
    stat = jnp.clip(jax.random.normal(key_b, (PAIRS, D), jnp.float32), -6.0, 6.0)
    return (stat, prem)


def draw_states(key, part):
    return pair_fields(key)[0].astype(jnp.bfloat16)


def draw_premises(key, part):
    return pair_fields(key)[1].astype(jnp.bfloat16)


def draw_counts(key, part):
    key_a, key_b = jax.random.split(jax.random.fold_in(key, 5))
    drawn = jax.random.randint(key_a, (N_LOOP * N_GROUPS,), TOK_DEV // 2, TOK_DEV + 1)
    where_full = jax.random.randint(key_b, (), 0, N_LOOP * N_GROUPS)
    drawn = drawn.at[where_full].set(TOK_DEV)
    return drawn.reshape(N_LOOP, N_GROUPS).astype(jnp.int32)


def draw_partner_mask(key, part):
    drawn = jax.random.randint(jax.random.fold_in(key, 23), (N_LOOP,), 0, N_GROUPS)
    drawn = drawn.at[0].set(N_GROUPS // 2)
    return drawn.astype(jnp.int32)


def touch_ends(values, rng, low, largest):
    spot = [jax.random.randint(jax.random.fold_in(rng, axis), (), 0, length) for axis, length in enumerate(values.shape)]
    widest = values.shape.index(max(values.shape))
    neighbour = spot[:widest] + [(spot[widest] + 1) % values.shape[widest]] + spot[widest + 1:]
    return values.at[tuple(spot)].set(low).at[tuple(neighbour)].set(largest)


def setup_inputs(seed: int = 0) -> dict:
    arg_keys = jax.random.split(jax.random.key(seed), 7)
    states = draw_states(jax.random.fold_in(arg_keys[6], 71), 0)
    premises = draw_premises(jax.random.fold_in(arg_keys[6], 71), 0)
    counts = draw_counts(jax.random.fold_in(arg_keys[6], 71), 0)
    partner_mask = draw_partner_mask(jax.random.fold_in(arg_keys[6], 71), 0)
    send_rows = touch_ends(jax.random.randint(arg_keys[4], (N_LOOP, N_GROUPS, HARD), 0, TOK_DEV // 2), jax.random.fold_in(arg_keys[4], 1), 0, (TOK_DEV // 2) - 1).astype(jnp.int32)
    hard_idx = touch_ends(jax.random.randint(arg_keys[5], (PAIRS,), 0, HARD), jax.random.fold_in(arg_keys[5], 1), 0, HARD - 1).astype(jnp.int32)
    return dict(states=states, premises=premises, counts=counts, partner_mask=partner_mask, send_rows=send_rows, hard_idx=hard_idx)


SCALE = 3.0


def reference(states, premises, counts, partner_mask, send_rows, hard_idx):
    width = states.shape[1]
    sfull = states.reshape(N_LOOP, N_GROUPS, TOK_DEV, width)
    qfull = premises.reshape(N_LOOP, N_GROUPS, TOK_DEV, width)
    index = hard_idx.reshape(N_LOOP, N_GROUPS, TOK_DEV)
    valid = jnp.arange(TOK_DEV, dtype=jnp.int32)[None, None, :] < counts[:, :, None]
    vflt = valid.astype(jnp.float32)
    gidx = jnp.arange(N_GROUPS, dtype=jnp.int32)
    partner = jnp.bitwise_xor(gidx[None, :], partner_mask[:, None]).astype(jnp.int32)
    offered = jnp.take_along_axis(qfull, send_rows[:, :, :, None], axis=2)
    pool = jnp.take_along_axis(offered, partner[:, :, None, None], axis=1)
    hard = jnp.take_along_axis(pool, index[:, :, :, None], axis=2)
    tval = SCALE * jnp.sum(sfull.astype(jnp.float32) * hard.astype(jnp.float32), axis=-1)

    sgrp = jnp.transpose(sfull, (1, 0, 2, 3)).reshape(N_GROUPS, N_LOOP * TOK_DEV, width)
    qgrp = jnp.transpose(qfull, (1, 0, 2, 3)).reshape(N_GROUPS, N_LOOP * TOK_DEV, width)
    vgrp = jnp.transpose(valid, (1, 0, 2)).reshape(N_GROUPS, N_LOOP * TOK_DEV)

    def one_group(item):
        sg, qg, vg = item
        scores = SCALE * jnp.dot(sg, qg.T, preferred_element_type=jnp.float32)
        masked = jnp.where(vg[None, :], scores, -jnp.inf)
        top = jnp.max(masked, axis=1)
        lse = top + jnp.log(jnp.sum(jnp.exp(masked - top[:, None]), axis=1))
        pos = jnp.diagonal(scores)
        prob = jnp.where(vg[:, None], jnp.exp(masked - lse[:, None]), 0.0).astype(jnp.bfloat16)
        dstate = jnp.dot(prob, qg, preferred_element_type=jnp.float32)
        dprem = jnp.dot(prob.T, sg, preferred_element_type=jnp.float32)
        return lse, pos, dstate, dprem

    lse, pos, dstate, dprem = lax.map(one_group, (sgrp, qgrp, vgrp))

    def regroup(arr):
        shaped = arr.reshape((N_GROUPS, N_LOOP, TOK_DEV) + arr.shape[2:])
        return jnp.swapaxes(shaped, 0, 1)

    lse = regroup(lse)
    pos = regroup(pos)
    dstate = regroup(dstate)
    dprem = regroup(dprem)
    qval = jnp.where(valid, jax.nn.sigmoid(tval - pos), 0.0)
    terms = jnp.where(valid, lse - pos + jax.nn.softplus(tval - pos), 0.0)
    loss = jnp.sum(terms) / (N_LOOP * N_GROUPS * TOK_DEV)
    grad_states = SCALE * (dstate + qval[..., None] * hard.astype(jnp.float32)
                           - (vflt + qval)[..., None] * qfull.astype(jnp.float32))
    pick = jax.nn.one_hot(index, HARD, dtype=jnp.float32)
    back = SCALE * jnp.einsum("lgpk,lgpd->lgkd", pick, qval[..., None] * sfull.astype(jnp.float32),
                              precision=lax.Precision.HIGHEST)
    back_home = jnp.take_along_axis(back, partner[:, :, None, None], axis=1)
    place = jax.nn.one_hot(send_rows, TOK_DEV, dtype=jnp.float32)
    dhard = jnp.einsum("lgkp,lgkd->lgpd", place, back_home, precision=lax.Precision.HIGHEST)
    grad_premises = dprem - SCALE * (vflt + qval)[..., None] * sfull.astype(jnp.float32) + dhard
    total = N_LOOP * N_GROUPS * TOK_DEV
    return (loss,
            grad_states.reshape(total, width).astype(jnp.bfloat16),
            grad_premises.reshape(total, width).astype(jnp.bfloat16))
```

```python
import functools

import jax
import jax.numpy as jnp
from jax import lax
from jax.experimental import pallas as pl
from jax.experimental.pallas import tpu as pltpu
from jax.sharding import PartitionSpec as P

SCALE = 3.0
LANES = 128
F32 = jnp.float32
BF16 = jnp.bfloat16
VMEM = pl.BlockSpec(memory_space=pltpu.VMEM)
SMEM = pl.BlockSpec(memory_space=pltpu.SMEM)
PARAMS = pltpu.CompilerParams(vmem_limit_bytes=40 << 20)


def swap(block, axis, mask):
    count = lax.axis_size(axis)
    return lax.ppermute(block, axis, [(i, i ^ mask) for i in range(count)])


def dot(a, b, dims):
    return lax.dot_general(a, b, (dims, ((), ())), preferred_element_type=F32)


def total(x):
    return jnp.sum(jnp.sum(x, axis=0, keepdims=True), axis=1, keepdims=True)


def parts(x):
    hi = x.astype(BF16)
    rest = x - hi.astype(F32)
    mid = rest.astype(BF16)
    low = (rest - mid.astype(F32)).astype(BF16)
    return hi, mid, low


def place_of(rows, picked):
    slot = lax.broadcasted_iota(jnp.int32, (rows, picked.shape[1]), 0)
    return jnp.where(slot == picked, 1.0, 0.0).astype(BF16)


def pack(message, block, scalar):
    width = block.shape[1]
    message[:, :width] = block.astype(BF16)
    for i, piece in enumerate(parts(jnp.broadcast_to(scalar, (block.shape[0], LANES)))):
        message[:, width + i * LANES : width + (i + 1) * LANES] = piece


def unpack(message):
    width = message.shape[1] - 3 * LANES
    pieces = [
        message[:, width + i * LANES : width + (i + 1) * LANES].astype(F32)
        for i in range(3)
    ]
    return message[:, :width], (pieces[0] + pieces[1] + pieces[2])[0:1, 0:1]


def merge_kernel(level, mine, other, mask, out, summed):
    block, scalar = unpack(mine)
    other_block, other_scalar = unpack(other)
    take = mask[0] >> level & 1
    block = jnp.where(jnp.full(block.shape, take, jnp.int32) == 1, other_block, block)
    scalar = scalar + other_scalar
    pack(out, block, scalar)
    summed[...] = jnp.broadcast_to(scalar, summed.shape)


def offer_kernel(premises, send_rows, counts, offered, limit):
    place = place_of(premises.shape[0], send_rows[...])
    offered[...] = dot(place, premises[...], ((0,), (0,))).astype(BF16)
    limit[...] = jnp.full(limit.shape, counts[0, 0], jnp.int32)


def hard_kernel(states, premises, pool, hard_idx, counts, qval, back, soft):
    rows, offer = states.shape[0], pool.shape[0]
    which = lax.broadcasted_iota(jnp.int32, (offer, rows), 0)
    pick = jnp.where(which == hard_idx[...], 1.0, 0.0)
    hard = dot(pick.astype(BF16), pool[...], ((0,), (0,)))
    states_f = states[...].astype(F32)
    tval = SCALE * jnp.sum(states_f * hard, axis=1, keepdims=True)
    pos = SCALE * jnp.sum(states_f * premises[...].astype(F32), axis=1, keepdims=True)
    valid = lax.broadcasted_iota(jnp.int32, (rows, 1), 0) < counts[0, 0]
    gap = tval - pos
    q = jnp.where(valid, 1.0 / (1.0 + jnp.exp(-gap)), 0.0)
    plus = jnp.maximum(gap, 0.0) + jnp.log(1.0 + jnp.exp(-jnp.abs(gap)))
    qval[...] = jnp.broadcast_to(q, qval.shape)
    soft[...] = jnp.broadcast_to(total(jnp.where(valid, plus - pos, 0.0)), soft.shape)
    weight = jnp.broadcast_to(q, (rows, rows)).T[:offer] * pick
    split = jnp.concatenate(parts(weight), axis=0)
    summed = dot(split, states[...], ((1,), (0,)))
    back[...] = SCALE * (
        summed[:offer] + summed[offer : 2 * offer] + summed[2 * offer :]
    )


def softmax(rows_block, keys, limits):
    rows = keys[0].shape[0]
    column = lax.broadcasted_iota(jnp.int32, (1, rows), 1)
    scores = []
    top = None
    for key, limit in zip(keys, limits):
        block = SCALE * dot(rows_block, key[...], ((1,), (1,)))
        block = jnp.where(column < limit[0:1, :], block, -jnp.inf)
        scores.append(block)
        best = jnp.max(block, axis=1, keepdims=True)
        top = best if top is None else jnp.maximum(top, best)
    weights = [jnp.exp(block - top) for block in scores]
    mass = sum(jnp.sum(w, axis=1, keepdims=True) for w in weights)
    return weights, top + jnp.log(mass), 1.0 / mass


def near_kernel(size, *refs):
    keys, limits = refs[:size], refs[size : 2 * size]
    own, sib, soft, soft_sib, back, prob, prob_sib, message = refs[2 * size :]
    rows = own.shape[0]
    slot = lax.broadcasted_iota(jnp.int32, (rows, 1), 0)
    summed = soft[0:1, 0:1] + soft_sib[0:1, 0:1]
    for block, limit, which in ((own, limits[0], 0), (sib, limits[1], 1)):
        weights, lse, inverse = softmax(block[...], keys, limits)
        valid = slot < limit[0:1, 0:1]
        summed = summed + total(jnp.where(valid, lse, 0.0))
        scale = jnp.where(valid, inverse, 0.0)
        if which == 0:
            for b in range(size):
                prob[:, b * rows : (b + 1) * rows] = (weights[b] * scale).astype(BF16)
        else:
            prob_sib[...] = (weights[0] * scale).astype(BF16)
    pack(message, back[...], summed)


def states_kernel(size, *refs):
    keys = refs[:size]
    prob, pool, hard_idx, qval, counts, out = refs[size:]
    rows, offer = keys[0].shape[0], pool.shape[0]
    grad = None
    for b in range(size):
        piece = dot(prob[:, b * rows : (b + 1) * rows], keys[b][...], ((1,), (0,)))
        grad = piece if grad is None else grad + piece
    which = lax.broadcasted_iota(jnp.int32, (offer, rows), 0)
    pick = jnp.where(which == hard_idx[...], 1.0, 0.0).astype(BF16)
    hard = dot(pick, pool[...], ((0,), (0,)))
    valid = lax.broadcasted_iota(jnp.int32, (rows, 1), 0) < counts[0, 0]
    q = qval[:, 0:1]
    vq = jnp.where(valid, 1.0, 0.0) + q
    grad = grad + q * hard - vq * keys[0][...].astype(F32)
    out[...] = (SCALE * grad).astype(BF16)


def premises_kernel(size, *refs):
    keys, limits, states = refs[:size], refs[size : 2 * size], refs[2 * size : 3 * size]
    prob, prob_sib, qval, counts, out = refs[3 * size :]
    rows = keys[0].shape[0]
    slot = lax.broadcasted_iota(jnp.int32, (rows, 1), 0)
    grad = dot(prob[:, :rows], states[0][...], ((0,), (0,)))
    grad = grad + dot(prob_sib[...], states[1][...], ((0,), (0,)))
    for b in range(2, size):
        weights, _, inverse = softmax(states[b][...], keys, limits)
        scale = jnp.where(slot < limits[b][0:1, 0:1], inverse, 0.0)
        mine = (weights[0] * scale).astype(BF16)
        grad = grad + dot(mine, states[b][...], ((0,), (0,)))
    vq = jnp.where(slot < counts[0, 0], 1.0, 0.0) + qval[:, 0:1]
    out[...] = grad - SCALE * vq * states[0][...].astype(F32)


def finish_kernel(grad, home, send_rows, out):
    place = place_of(grad.shape[0], send_rows[...])
    out[...] = (grad[...] + dot(place, home[...], ((1,), (0,)))).astype(BF16)


def shape(dims, dtype):
    return jax.ShapeDtypeStruct(dims, dtype)


def spread(held, bits):
    for bit in reversed(range(bits - 1)):
        for m in list(held):
            if m | 1 << bit not in held:
                held[m | 1 << bit] = swap(held[m], "loop", 1 << bit)


def body(states, premises, counts, partner_mask, send_rows, hard_idx):
    rows, width = states.shape
    offer = send_rows.shape[2]
    loop_size = lax.axis_size("loop")
    group_size = lax.axis_size("groups")
    loop_bits = loop_size.bit_length() - 1
    group_bits = group_size.bit_length() - 1
    mask = partner_mask[0]
    sent = send_rows[0]
    index = hard_idx[None, :]

    def after(value, *earlier):
        return lax.optimization_barrier((value, *earlier))[0]

    keys = {0: premises}
    all_states = {0: states}
    top_bit = 1 << (loop_bits - 1)
    keys[top_bit] = swap(premises, "loop", top_bit)
    all_states[top_bit] = swap(states, "loop", top_bit)
    offered, limit = pl.pallas_call(
        offer_kernel,
        out_shape=(shape((offer, width), BF16), shape((8, rows), jnp.int32)),
        in_specs=[VMEM, VMEM, SMEM],
        out_specs=(VMEM, VMEM),
        compiler_params=PARAMS,
        name="offer",
    )(premises, sent, counts)
    limits = {0: limit, top_bit: swap(limit, "loop", top_bit)}

    def route(m):
        return lambda block: block if m == 0 else swap(block, "groups", m)

    pool = lax.switch(mask, [route(m) for m in range(group_size)], offered)

    qval, back, soft = pl.pallas_call(
        hard_kernel,
        out_shape=(
            shape((rows, LANES), F32),
            shape((offer, width), F32),
            shape((8, LANES), F32),
        ),
        in_specs=[VMEM] * 4 + [SMEM],
        out_specs=(VMEM,) * 3,
        compiler_params=PARAMS,
        name="hard",
    )(states, premises, pool, index, counts)
    soft_sib = swap(soft, "loop", 1)
    keys[top_bit] = after(keys[top_bit], soft)
    spread(limits, loop_bits)
    spread(keys, loop_bits)
    keys = [keys[m] for m in range(loop_size)]
    limits = [limits[m] for m in range(loop_size)]
    states_sib = swap(states, "loop", 1)

    prob, prob_sib, message = pl.pallas_call(
        functools.partial(near_kernel, loop_size),
        out_shape=(
            shape((rows, loop_size * rows), BF16),
            shape((rows, rows), BF16),
            shape((offer, width + 3 * LANES), BF16),
        ),
        in_specs=[VMEM] * (2 * loop_size + 5),
        out_specs=(VMEM,) * 3,
        compiler_params=PARAMS,
        name="near",
    )(*keys, *limits, states, states_sib, soft, soft_sib, back)

    for level in range(group_bits):
        message, part = pl.pallas_call(
            functools.partial(merge_kernel, level),
            out_shape=(shape(message.shape, BF16), shape((8, LANES), F32)),
            in_specs=[VMEM, VMEM, SMEM],
            out_specs=(VMEM, VMEM),
            compiler_params=PARAMS,
            name="merge",
        )(message, swap(message, "groups", 1 << level), partner_mask)
    odd = lax.axis_index("loop") & 1

    def across(block):
        for bit in range(1, loop_bits):
            block = block + swap(block, "loop", 1 << bit)
        return block

    part = lax.cond(odd == 1, across, lambda block: block, part)
    part = jnp.where(odd == 1, part, swap(part, "loop", 1))
    loss = part[0, 0] / (loop_size * group_size * rows)
    home = message[:, :width]

    all_states[top_bit] = after(all_states[top_bit], prob)
    spread(all_states, loop_bits)
    all_states[1] = states_sib
    all_states = [all_states[m] for m in range(loop_size)]
    grad_states = pl.pallas_call(
        functools.partial(states_kernel, loop_size),
        out_shape=shape((rows, width), BF16),
        in_specs=[VMEM] * (loop_size + 4) + [SMEM],
        out_specs=VMEM,
        compiler_params=PARAMS,
        name="states",
    )(*keys, prob, pool, index, qval, counts)
    partial_grad = pl.pallas_call(
        functools.partial(premises_kernel, loop_size),
        out_shape=shape((rows, width), F32),
        in_specs=[VMEM] * (3 * loop_size + 3) + [SMEM],
        out_specs=VMEM,
        compiler_params=PARAMS,
        name="premises",
    )(*keys, *limits, *all_states, prob, prob_sib, qval, counts)
    grad_premises = pl.pallas_call(
        finish_kernel,
        out_shape=shape((rows, width), BF16),
        in_specs=[VMEM] * 3,
        out_specs=VMEM,
        compiler_params=PARAMS,
        name="finish",
    )(partial_grad, home, sent)
    return loss, grad_states, grad_premises


def solution(mesh):
    return jax.shard_map(
        body,
        mesh=mesh,
        in_specs=(
            P(("loop", "groups"), None),
            P(("loop", "groups"), None),
            P("loop", "groups"),
            P("loop"),
            P("loop", "groups", None),
            P(("loop", "groups")),
        ),
        out_specs=(P(), P(("loop", "groups"), None), P(("loop", "groups"), None)),
        check_vma=False,
    )
```

```python
import functools

import jax
import jax.numpy as jnp
from jax import lax
from jax.experimental import pallas as pl
from jax.experimental.pallas import tpu as pltpu
from jax.sharding import PartitionSpec as P

SCALE = 3.0
LANES = 128
F32 = jnp.float32
BF16 = jnp.bfloat16
VMEM = pl.BlockSpec(memory_space=pltpu.VMEM)
SMEM = pl.BlockSpec(memory_space=pltpu.SMEM)
HBM = pl.BlockSpec(memory_space=pltpu.HBM)


def swap(block, axis, mask):
    count = lax.axis_size(axis)
    return lax.ppermute(block, axis, [(i, i ^ mask) for i in range(count)])


def shape(dims, dtype=BF16):
    return jax.ShapeDtypeStruct(dims, dtype)


def call(kernel, name, outs, *args, ins=None, out_specs=None, scratch=(), cost=0, vmem=40 << 20):
    ins = ins or {}
    return pl.pallas_call(
        kernel,
        out_shape=outs,
        in_specs=[ins.get(i, VMEM) for i in range(len(args))],
        out_specs=out_specs or jax.tree.map(lambda _: VMEM, outs),
        scratch_shapes=scratch,
        compiler_params=pltpu.CompilerParams(vmem_limit_bytes=vmem),
        cost_estimate=pl.CostEstimate(flops=0, bytes_accessed=cost, transcendentals=0),
        name=name,
    )(*args)


def dot(a, b, dims):
    return lax.dot_general(a, b, (dims, ((), ())), preferred_element_type=F32)


def total(x):
    return jnp.sum(jnp.sum(x, axis=0, keepdims=True), axis=1, keepdims=True)


def parts(x):
    hi = x.astype(BF16)
    rest = x - hi.astype(F32)
    mid = rest.astype(BF16)
    low = (rest - mid.astype(F32)).astype(BF16)
    return hi, mid, low


def place_of(rows, picked):
    slot = lax.broadcasted_iota(jnp.int32, (rows, picked.shape[1]), 0)
    return jnp.where(slot == picked, 1.0, 0.0).astype(BF16)


def pick_of(offer, hard_idx):
    which = lax.broadcasted_iota(jnp.int32, (offer, hard_idx.shape[1]), 0)
    return jnp.where(which == hard_idx, 1.0, 0.0)


def column(rows):
    return lax.broadcasted_iota(jnp.int32, (rows, 1), 0).astype(F32)


def pack(message, block, scalar):
    offer, width = block.shape
    message[:, :width] = block.astype(BF16)
    row = lax.broadcasted_iota(jnp.int32, (offer, LANES), 0)
    hi, mid, low = (p.astype(F32) for p in parts(jnp.broadcast_to(scalar, row.shape)))
    spread = jnp.where(row == 0, hi, jnp.where(row == 1, mid, jnp.where(row == 2, low, 0.0)))
    message[:, width:] = spread.astype(BF16)


def unpack(message):
    width = message.shape[1] - LANES
    spread = message[:, width:].astype(F32)
    return message[:, :width], jnp.sum(spread, axis=0, keepdims=True)[:, 0:1]


def mark_kernel(premises, count, marked, held, sem):
    copy = pltpu.make_async_copy(premises, held, sem)
    copy.start()
    copy.wait()
    rows = premises.shape[0]
    row = lax.broadcasted_iota(jnp.int32, (rows, LANES), 0)
    lane = lax.broadcasted_iota(jnp.int32, (rows, LANES), 1)
    invalid = jnp.logical_and(row >= count[0, 0], lane == 0)
    marked[:, LANES:] = held[:, LANES:]
    marked[:, :LANES] = jnp.where(invalid, jnp.inf, held[:, :LANES].astype(F32)).astype(BF16)


def is_valid(key):
    return key[:, 0:1].astype(F32) < jnp.inf


def count_of(meta):
    return meta[3:4, 0:1].astype(F32)


def front_kernel(size, *refs):
    sources, (offered, meta), held = refs[:size], refs[size : size + 2], refs[size + 2 : -1]
    sems = refs[-1]
    copies = [
        pltpu.make_async_copy(source, target, sems.at[i])
        for i, (source, target) in enumerate(zip(sources, held))
    ]
    for copy in copies:
        copy.start()
    for copy in copies:
        copy.wait()
    premises, send_rows, hard_idx, mask, counts = held
    row = lax.broadcasted_iota(jnp.int32, meta.shape, 0)
    meta[...] = jnp.where(
        row == 0, hard_idx[...], jnp.where(row == 2, mask[...], counts[...])
    )
    meta[1:2, 0 : send_rows.shape[1]] = send_rows[...]
    place = place_of(premises.shape[0], send_rows[...])
    offered[...] = dot(place, premises[...], ((0,), (0,))).astype(BF16)


def hard_kernel(states, premises, pool, meta, qval, back, soft):
    rows, offer = states.shape[0], pool.shape[0]
    pick = pick_of(offer, meta[0:1, :])
    hard = dot(pick.astype(BF16), pool[...], ((0,), (0,)))
    states_f = states[...].astype(F32)
    tval = SCALE * jnp.sum(states_f * hard, axis=1, keepdims=True)
    pos = SCALE * jnp.sum(states_f * premises[...].astype(F32), axis=1, keepdims=True)
    valid = column(rows) < count_of(meta)
    gap = tval - pos
    q = jnp.where(valid, 1.0 / (1.0 + jnp.exp(-gap)), 0.0)
    plus = jnp.maximum(gap, 0.0) + jnp.log(1.0 + jnp.exp(-jnp.abs(gap)))
    qval[...] = jnp.broadcast_to(q, qval.shape)
    soft[...] = jnp.broadcast_to(total(jnp.where(valid, plus - pos, 0.0)), soft.shape)
    weight = jnp.broadcast_to(q, (rows, rows)).T[:offer] * pick
    split = jnp.concatenate(parts(weight), axis=0)
    summed = dot(split, states[...], ((1,), (0,)))
    summed = summed[:offer] + summed[offer : 2 * offer] + summed[2 * offer :]
    back[...] = (SCALE * summed).astype(BF16)


def line(width):
    return lax.broadcasted_iota(jnp.int32, (1, width), 1).astype(F32)


def mask_keys(scores, ok):
    return jnp.where(ok, scores, -jnp.inf)


def score(key, block, limit):
    return mask_keys(SCALE * dot(key, block, ((1,), (1,))), column(key.shape[0]) < limit)


def tops(blocks):
    return jnp.max(functools.reduce(jnp.maximum, blocks), axis=0, keepdims=True)


def masses(blocks, top):
    weights = functools.reduce(jnp.add, [jnp.exp(block - top) for block in blocks])
    return jnp.sum(weights, axis=0, keepdims=True)


def early_kernel(size, own, sib, soft, *refs):
    keys, stats = refs[:size], refs[size]
    rows = own.shape[0]
    both = jnp.concatenate([own[...], sib[...]], axis=0)
    oks = [is_valid(key) for key in keys]
    blocks = [mask_keys(SCALE * dot(key[...], both, ((1,), (1,))), ok) for key, ok in zip(keys, oks)]
    top = tops(blocks)
    stats[0:1, :] = top
    stats[1:2, :] = masses(blocks, top)
    info = jnp.broadcast_to(soft[0:1, 0:1], (1, stats.shape[1]))
    for i, ok in enumerate(oks):
        info = jnp.where(line(stats.shape[1]) == 1 + i, total(jnp.where(ok, 1.0, 0.0)), info)
    stats[2:3, :] = info


def limit_of(stats, stats_sib, m):
    return (stats_sib if m & 1 else stats)[2:3, 1 + (m >> 1) : 2 + (m >> 1)]


def valid_lanes(stats, stats_sib, m, rows):
    slots = line(rows)
    pair = [slots < limit_of(stats, stats_sib, m + i) for i in range(2)]
    return jnp.concatenate(pair, axis=1)


def near_kernel(stats, stats_sib, back, lse, message):
    rows = stats.shape[1] // 2
    top, mass = stats[0:1, :], stats[1:2, :]
    flip = [
        jnp.concatenate([stats_sib[i : i + 1, rows:], stats_sib[i : i + 1, :rows]], axis=1)
        for i in range(2)
    ]
    best = jnp.maximum(top, flip[0])
    mass = mass * jnp.exp(top - best) + flip[1] * jnp.exp(flip[0] - best)
    out = best + jnp.log(mass)
    lse[...] = jnp.broadcast_to(out, lse.shape)
    out = jnp.where(valid_lanes(stats, stats_sib, 0, rows), out, 0.0)
    pack(message, back[...], total(out) + stats[2:3, 0:1] + stats_sib[2:3, 0:1])


def merge_kernel(level, last, mine, other, meta, *outs):
    block, scalar = unpack(mine)
    other_block, other_scalar = unpack(other)
    take = meta[2:3, 0:1] >> level & 1
    block = jnp.where(take == 1, other_block.astype(F32), block.astype(F32)).astype(BF16)
    scalar = scalar + other_scalar
    if last:
        outs[0][...] = block
        outs[1][...] = jnp.broadcast_to(scalar, outs[1].shape)
    else:
        pack(outs[0], block, scalar)


def states_kernel(size, *refs):
    keys = refs[:size]
    states, lse, pool, meta, qval, stats, stats_sib, out = refs[size:]
    rows, offer = states.shape[0], pool.shape[0]
    slot = column(rows)
    valid = slot < count_of(meta)
    limits = [limit_of(stats, stats_sib, m) for m in range(size)]
    cleared = [keys[0][...]] + [
        jnp.where(slot < limit, key[...].astype(F32), 0.0).astype(BF16)
        for key, limit in zip(keys[1:], limits[1:])
    ]
    cleared = jnp.concatenate(cleared, axis=0)
    scores = SCALE * dot(states[...], cleared, ((1,), (1,)))
    lse_column = jnp.broadcast_to(lse[0:1, :rows], (rows, rows)).T[:, 0:1]
    ok = jnp.concatenate([line(rows) < limit for limit in limits], axis=1)
    prob = jnp.where(jnp.logical_and(valid, ok), jnp.exp(scores - lse_column), 0.0)
    grad = dot(prob.astype(BF16), cleared, ((1,), (0,)))
    hard = dot(pick_of(offer, meta[0:1, :]).astype(BF16), pool[...], ((0,), (0,)))
    q = qval[:, 0:1]
    vq = jnp.where(valid, 1.0, 0.0) + q
    grad = grad + q * hard - vq * keys[0][...].astype(F32)
    out[...] = (SCALE * grad).astype(BF16)


def premises_kernel(size, *refs):
    keys, states = refs[:size], refs[size : 2 * size]
    lse, meta, qval, stats, stats_sib, out = refs[2 * size :]
    rows = states[0].shape[0]
    grad = None
    for b in range(0, size, 2):
        both = jnp.concatenate([states[b][...], states[b + 1][...]], axis=0)
        mine = score(keys[0][...], both, count_of(meta))
        if b == 0:
            total_lse = lse[0:1, :]
        else:
            blocks = [mine] + [
                score(keys[m][...], both, limit_of(stats, stats_sib, m))
                for m in range(1, size)
            ]
            top = tops(blocks)
            total_lse = top + jnp.log(masses(blocks, top))
        row_ok = valid_lanes(stats, stats_sib, b, rows)
        prob = jnp.where(row_ok, jnp.exp(mine - total_lse), 0.0).astype(BF16)
        piece = dot(prob, both, ((1,), (0,)))
        grad = piece if grad is None else grad + piece
    vq = jnp.where(column(rows) < count_of(meta), 1.0, 0.0) + qval[:, 0:1]
    out[...] = grad - SCALE * vq * states[0][...].astype(F32)


def finish_kernel(count, grad_states, grad, home, meta, part, other, out_states, out, loss):
    place = place_of(grad.shape[0], meta[1:2, 0 : home.shape[0]])
    out[...] = (grad[...] + dot(place, home[...], ((1,), (0,)))).astype(BF16)
    out_states[...] = grad_states[...]
    odd = jnp.full((1, 1), lax.axis_index("loop") & 1, jnp.int32) == 1
    loss[...] = jnp.where(odd, part[0:1, 0:1], other[0:1, 0:1]) / count


def across_chips(held, bits):
    for bit in reversed(range(1, bits)):
        held.update({m | 1 << bit: swap(b, "loop", 1 << bit) for m, b in held.items()})
    return held


def from_sibling(held):
    for m in [m for m in held if not m & 1 and m | 1 not in held]:
        held[m | 1] = swap(held[m], "loop", 1)
    return [held[m] for m in range(len(held))]


def body(states, premises, counts, partner_mask, send_rows, hard_idx):
    rows, width = states.shape
    offer = send_rows.shape[2]
    loop_size = lax.axis_size("loop")
    group_size = lax.axis_size("groups")
    loop_bits = loop_size.bit_length() - 1
    group_bits = group_size.bit_length() - 1

    def after(value, *earlier):
        return lax.optimization_barrier((value, *earlier))[0] if earlier else value

    sources = (premises, send_rows[0], hard_idx[None, :], partner_mask[None, :], counts)
    marked = call(
        mark_kernel,
        "mark",
        shape((rows, width)),
        premises,
        counts,
        ins={0: HBM, 1: SMEM},
        scratch=[pltpu.VMEM((rows, width), BF16), pltpu.SemaphoreType.DMA(())],
        vmem=40 << 20,
    )
    offered, meta = call(
        functools.partial(front_kernel, len(sources)),
        "front",
        (shape((offer, width)), shape((8, rows), jnp.int32)),
        *sources,
        ins={i: HBM for i in range(len(sources))},
        scratch=[pltpu.VMEM(source.shape, source.dtype) for source in sources]
        + [pltpu.SemaphoreType.DMA((len(sources),))],
        vmem=40 << 20,
    )
    keys = across_chips({0: marked}, loop_bits)
    states_sib = swap(after(states, marked), "loop", 1)

    def route(m):
        return lambda block: block if m == 0 else swap(block, "groups", m)

    pool = lax.switch(partner_mask[0], [route(m) for m in range(group_size)], offered)

    qval, back, soft = call(
        hard_kernel,
        "hard",
        (shape((rows, LANES), F32), shape((offer, width)), shape((8, LANES), F32)),
        states,
        premises,
        pool,
        meta,
    )
    even = range(0, loop_size, 2)
    for m in even:
        if m:
            keys[m] = after(keys[m], back)
    states_sib, keys_sib = lax.optimization_barrier(
        (states_sib, swap(marked, "loop", 1))
    )
    stats = call(
        functools.partial(early_kernel, len(even)),
        "early",
        shape((8, 2 * rows), F32),
        states,
        states_sib,
        soft,
        *(keys[m] for m in even),
    )
    stats_sib = swap(stats, "loop", 1)
    lse, message = call(
        near_kernel,
        "near",
        (shape((8, 2 * rows), F32), shape((offer, width + LANES))),
        stats,
        stats_sib,
        back,
    )
    for m in even:
        keys[m] = after(keys[m], stats)
    keys[1] = keys_sib
    keys = from_sibling(keys)
    keys[0] = premises
    grad_states = call(
        functools.partial(states_kernel, loop_size),
        "states",
        shape((rows, width)),
        *keys,
        states,
        lse,
        pool,
        meta,
        qval,
        stats,
        stats_sib,
        cost=1 << 22,
    )
    all_states = across_chips({0: after(states, marked)}, loop_bits)
    for level in range(group_bits):
        last = level == group_bits - 1
        outs = (shape((offer, width)), shape((8, LANES), F32))
        other = swap(message, "groups", 1 << level)
        if level == 1:
            other = after(other, grad_states)
        if level == 2:
            other = after(other, grad)
        message = call(
            functools.partial(merge_kernel, level, last),
            "merge",
            outs if last else shape(message.shape),
            message,
            other,
            meta,
        )
        if level == 0:
            for m in even:
                if m:
                    all_states[m] = after(all_states[m], message)
            all_states[1] = states_sib
            all_states = from_sibling(all_states)
            grad = call(
                functools.partial(premises_kernel, loop_size),
                "premises",
                shape((rows, width), F32),
                *keys,
                *all_states,
                lse,
                meta,
                qval,
                stats,
                stats_sib,
                cost=1 << 22,
            )
    home, part = message
    odd = lax.axis_index("loop") & 1

    def across(block):
        for bit in range(1, loop_bits):
            block = block + swap(block, "loop", 1 << bit)
        return block

    part = lax.cond(odd == 1, across, lambda block: block, part)
    grad_states, grad_premises, loss = call(
        functools.partial(finish_kernel, loop_size * group_size * rows),
        "finish",
        (shape((rows, width)), shape((rows, width)), shape((1, 1), F32)),
        grad_states,
        grad,
        home,
        meta,
        part,
        swap(part, "loop", 1),
    )
    return loss[0, 0], grad_states, grad_premises


def solution(mesh):
    return jax.shard_map(
        body,
        mesh=mesh,
        in_specs=(
            P(("loop", "groups"), None),
            P(("loop", "groups"), None),
            P("loop", "groups"),
            P("loop"),
            P("loop", "groups", None),
            P(("loop", "groups")),
        ),
        out_specs=(P(), P(("loop", "groups"), None), P(("loop", "groups"), None)),
        check_vma=False,
    )
```

```python
import functools

import jax
import jax.numpy as jnp
from jax import lax
from jax.experimental import pallas as pl
from jax.experimental.pallas import tpu as pltpu
from jax.sharding import PartitionSpec as P

SCALE = 3.0
LANES = 128
F32 = jnp.float32
BF16 = jnp.bfloat16
VMEM = pl.BlockSpec(memory_space=pltpu.VMEM)
SMEM = pl.BlockSpec(memory_space=pltpu.SMEM)
HBM = pl.BlockSpec(memory_space=pltpu.HBM)


def swap(block, axis, mask):
    count = lax.axis_size(axis)
    return lax.ppermute(block, axis, [(i, i ^ mask) for i in range(count)])


def shape(dims, dtype=BF16):
    return jax.ShapeDtypeStruct(dims, dtype)


def call(kernel, name, outs, *args, ins=None, out_specs=None, scratch=(), cost=0, vmem=40 << 20):
    ins = ins or {}
    return pl.pallas_call(
        kernel,
        out_shape=outs,
        in_specs=[ins.get(i, VMEM) for i in range(len(args))],
        out_specs=out_specs or jax.tree.map(lambda _: VMEM, outs),
        scratch_shapes=scratch,
        compiler_params=pltpu.CompilerParams(vmem_limit_bytes=vmem),
        cost_estimate=pl.CostEstimate(flops=cost, bytes_accessed=0, transcendentals=0),
        name=name,
    )(*args)


def dot(a, b, dims):
    return lax.dot_general(a, b, (dims, ((), ())), preferred_element_type=F32)


def total(x):
    return jnp.sum(jnp.sum(x, axis=0, keepdims=True), axis=1, keepdims=True)


def parts(x):
    hi = x.astype(BF16)
    rest = x - hi.astype(F32)
    mid = rest.astype(BF16)
    low = (rest - mid.astype(F32)).astype(BF16)
    return hi, mid, low


def place_of(rows, picked):
    slot = lax.broadcasted_iota(jnp.int32, (rows, picked.shape[1]), 0)
    return jnp.where(slot == picked, 1.0, 0.0).astype(BF16)


def pick_of(offer, hard_idx):
    which = lax.broadcasted_iota(jnp.int32, (offer, hard_idx.shape[1]), 0)
    return jnp.where(which == hard_idx, 1.0, 0.0)


def column(rows):
    return lax.broadcasted_iota(jnp.int32, (rows, 1), 0).astype(F32)


def pack(message, block, scalar):
    offer, width = block.shape
    message[:, :width] = block.astype(BF16)
    row = lax.broadcasted_iota(jnp.int32, (offer, LANES), 0)
    hi, mid, low = (p.astype(F32) for p in parts(jnp.broadcast_to(scalar, row.shape)))
    spread = jnp.where(row == 0, hi, jnp.where(row == 1, mid, jnp.where(row == 2, low, 0.0)))
    message[:, width:] = spread.astype(BF16)


def unpack(message):
    width = message.shape[1] - LANES
    spread = message[:, width:].astype(F32)
    return message[:, :width], jnp.sum(spread, axis=0, keepdims=True)[:, 0:1]


def mark_kernel(premises, count, marked, held, sem):
    copy = pltpu.make_async_copy(premises, held, sem)
    copy.start()
    copy.wait()
    rows = premises.shape[0]
    row = lax.broadcasted_iota(jnp.int32, (rows, LANES), 0)
    lane = lax.broadcasted_iota(jnp.int32, (rows, LANES), 1)
    invalid = jnp.logical_and(row >= count[0, 0], lane == 0)
    marked[:, LANES:] = held[:, LANES:]
    marked[:, :LANES] = jnp.where(invalid, jnp.inf, held[:, :LANES].astype(F32)).astype(BF16)


def is_valid(key):
    return key[:, 0:1].astype(F32) < jnp.inf


def count_of(meta):
    return meta[3:4, 0:1].astype(F32)


def front_kernel(size, *refs):
    sources, (offered, meta), held = refs[:size], refs[size : size + 2], refs[size + 2 : -1]
    sems = refs[-1]
    copies = [
        pltpu.make_async_copy(source, target, sems.at[i])
        for i, (source, target) in enumerate(zip(sources, held))
    ]
    for copy in copies:
        copy.start()
    for copy in copies:
        copy.wait()
    premises, send_rows, hard_idx, mask, counts = held
    row = lax.broadcasted_iota(jnp.int32, meta.shape, 0)
    meta[...] = jnp.where(
        row == 0, hard_idx[...], jnp.where(row == 2, mask[...], counts[...])
    )
    meta[1:2, 0 : send_rows.shape[1]] = send_rows[...]
    place = place_of(premises.shape[0], send_rows[...])
    offered[...] = dot(place, premises[...], ((0,), (0,))).astype(BF16)


def hard_kernel(states, premises, pool, meta, qval, soft):
    rows, offer = states.shape[0], pool.shape[0]
    pick = pick_of(offer, meta[0:1, :])
    hard = dot(pick.astype(BF16), pool[...], ((0,), (0,)))
    states_f = states[...].astype(F32)
    tval = SCALE * jnp.sum(states_f * hard, axis=1, keepdims=True)
    pos = SCALE * jnp.sum(states_f * premises[...].astype(F32), axis=1, keepdims=True)
    valid = column(rows) < count_of(meta)
    gap = tval - pos
    q = jnp.where(valid, 1.0 / (1.0 + jnp.exp(-gap)), 0.0)
    plus = jnp.maximum(gap, 0.0) + jnp.log(1.0 + jnp.exp(-jnp.abs(gap)))
    qval[...] = jnp.broadcast_to(q, qval.shape)
    soft[...] = jnp.broadcast_to(total(jnp.where(valid, plus - pos, 0.0)), soft.shape)


def back_kernel(states, qval, meta, back):
    offer = back.shape[0]
    weight = qval[...].T[:offer] * pick_of(offer, meta[0:1, :])
    split = jnp.concatenate(parts(weight), axis=0)
    summed = dot(split, states[...], ((1,), (0,)))
    summed = summed[:offer] + summed[offer : 2 * offer] + summed[2 * offer :]
    back[...] = (SCALE * summed).astype(BF16)


def line(width):
    return lax.broadcasted_iota(jnp.int32, (1, width), 1).astype(F32)


def mask_keys(scores, ok):
    return jnp.where(ok, scores, -jnp.inf)


def score(key, block, limit):
    return mask_keys(SCALE * dot(key, block, ((1,), (1,))), column(key.shape[0]) < limit)


def tops(blocks):
    return jnp.max(functools.reduce(jnp.maximum, blocks), axis=0, keepdims=True)


def masses(blocks, top):
    weights = functools.reduce(jnp.add, [jnp.exp(block - top) for block in blocks])
    return jnp.sum(weights, axis=0, keepdims=True)


def early_kernel(size, own, sib, soft, *refs):
    keys, stats = refs[:size], refs[size]
    rows = own.shape[0]
    both = jnp.concatenate([own[...], sib[...]], axis=0)
    oks = [is_valid(key) for key in keys]
    blocks = [mask_keys(SCALE * dot(key[...], both, ((1,), (1,))), ok) for key, ok in zip(keys, oks)]
    top = tops(blocks)
    stats[0:1, :] = top
    stats[1:2, :] = masses(blocks, top)
    info = jnp.broadcast_to(soft[0:1, 0:1], (1, stats.shape[1]))
    for i, ok in enumerate(oks):
        info = jnp.where(line(stats.shape[1]) == 1 + i, total(jnp.where(ok, 1.0, 0.0)), info)
    stats[2:3, :] = info


def limit_of(stats, stats_sib, m):
    return (stats_sib if m & 1 else stats)[2:3, 1 + (m >> 1) : 2 + (m >> 1)]


def valid_lanes(stats, stats_sib, m, rows):
    slots = line(rows)
    pair = [slots < limit_of(stats, stats_sib, m + i) for i in range(2)]
    return jnp.concatenate(pair, axis=1)


def near_kernel(stats, stats_sib, back, lse, message):
    rows = stats.shape[1] // 2
    top, mass = stats[0:1, :], stats[1:2, :]
    flip = [
        jnp.concatenate([stats_sib[i : i + 1, rows:], stats_sib[i : i + 1, :rows]], axis=1)
        for i in range(2)
    ]
    best = jnp.maximum(top, flip[0])
    mass = mass * jnp.exp(top - best) + flip[1] * jnp.exp(flip[0] - best)
    out = best + jnp.log(mass)
    lse[...] = jnp.broadcast_to(out, lse.shape)
    out = jnp.where(valid_lanes(stats, stats_sib, 0, rows), out, 0.0)
    pack(message, back[...], total(out) + stats[2:3, 0:1] + stats_sib[2:3, 0:1])


def merge_kernel(level, last, mine, other, meta, *outs):
    block, scalar = unpack(mine)
    other_block, other_scalar = unpack(other)
    take = meta[2:3, 0:1] >> level & 1
    block = jnp.where(take == 1, other_block.astype(F32), block.astype(F32)).astype(BF16)
    scalar = scalar + other_scalar
    if last:
        outs[0][...] = block
        outs[1][...] = jnp.broadcast_to(scalar, outs[1].shape)
    else:
        pack(outs[0], block, scalar)


def states_kernel(size, *refs):
    keys = refs[:size]
    states, lse, pool, meta, qval, stats, stats_sib, out = refs[size:]
    rows, offer = states.shape[0], pool.shape[0]
    slot = column(rows)
    valid = slot < count_of(meta)
    limits = [limit_of(stats, stats_sib, m) for m in range(size)]
    cleared = [keys[0][...]] + [
        jnp.where(slot < limit, key[...].astype(F32), 0.0).astype(BF16)
        for key, limit in zip(keys[1:], limits[1:])
    ]
    cleared = jnp.concatenate(cleared, axis=0)
    scores = SCALE * dot(states[...], cleared, ((1,), (1,)))
    lse_column = jnp.broadcast_to(lse[0:1, :rows], (rows, rows)).T[:, 0:1]
    ok = jnp.concatenate([line(rows) < limit for limit in limits], axis=1)
    prob = jnp.where(jnp.logical_and(valid, ok), jnp.exp(scores - lse_column), 0.0)
    grad = dot(prob.astype(BF16), cleared, ((1,), (0,)))
    hard = dot(pick_of(offer, meta[0:1, :]).astype(BF16), pool[...], ((0,), (0,)))
    q = qval[:, 0:1]
    vq = jnp.where(valid, 1.0, 0.0) + q
    grad = grad + q * hard - vq * keys[0][...].astype(F32)
    out[...] = (SCALE * grad).astype(BF16)


def premises_kernel(size, *refs):
    keys = refs[:size]
    own, sib, lse, qval, stats, stats_sib, near = refs[size : size + 7]
    far = refs[size + 7 :]
    rows = own.shape[0]
    both = jnp.concatenate([own[...], sib[...]], axis=0)
    row_ok = valid_lanes(stats, stats_sib, 0, rows)
    held = jnp.concatenate([key[...] for key in keys], axis=0)
    scores = SCALE * dot(held, both, ((1,), (1,)))
    ok = jnp.logical_and(is_valid(held), row_ok)
    prob = jnp.where(ok, jnp.exp(scores - lse[0:1, :]), 0.0).astype(BF16)
    grad = dot(prob, both, ((1,), (0,)))
    vq = jnp.where(is_valid(keys[0]), 1.0, 0.0) + qval[:, 0:1]
    near[...] = grad[:rows] - SCALE * vq * own[...].astype(F32)
    for i, out in enumerate(far):
        out[...] = grad[(i + 1) * rows : (i + 2) * rows].astype(BF16)


def finish_kernel(size, grad_states, grad, home, meta, *refs):
    far, (out_states, out) = refs[:size], refs[size:]
    place = place_of(grad.shape[0], meta[1:2, 0 : home.shape[0]])
    summed = grad[...] + dot(place, home[...], ((1,), (0,)))
    for block in far:
        summed = summed + block[...].astype(F32)
    out[...] = summed.astype(BF16)
    out_states[...] = grad_states[...]


def loss_kernel(count, part, other, out):
    odd = jnp.full((1, 1), lax.axis_index("loop") & 1, jnp.int32) == 1
    out[...] = jnp.where(odd, part[0:1, 0:1], other[0:1, 0:1]) / count


def across_chips(held, bits):
    for bit in reversed(range(1, bits)):
        held.update({m | 1 << bit: swap(b, "loop", 1 << bit) for m, b in held.items()})
    return held


def from_sibling(held):
    for m in [m for m in held if not m & 1 and m | 1 not in held]:
        held[m | 1] = swap(held[m], "loop", 1)
    return [held[m] for m in range(len(held))]


def body(states, premises, counts, partner_mask, send_rows, hard_idx):
    rows, width = states.shape
    offer = send_rows.shape[2]
    loop_size = lax.axis_size("loop")
    group_size = lax.axis_size("groups")
    loop_bits = loop_size.bit_length() - 1
    group_bits = group_size.bit_length() - 1

    def after(value, *earlier):
        return lax.optimization_barrier((value, *earlier))[0] if earlier else value

    sources = (premises, send_rows[0], hard_idx[None, :], partner_mask[None, :], counts)
    marked = call(
        mark_kernel,
        "mark",
        shape((rows, width)),
        premises,
        counts,
        ins={0: HBM, 1: SMEM},
        scratch=[pltpu.VMEM((rows, width), BF16), pltpu.SemaphoreType.DMA(())],
        vmem=40 << 20,
    )
    offered, meta = call(
        functools.partial(front_kernel, len(sources)),
        "front",
        (shape((offer, width)), shape((8, rows), jnp.int32)),
        *sources,
        ins={i: HBM for i in range(len(sources))},
        scratch=[pltpu.VMEM(source.shape, source.dtype) for source in sources]
        + [pltpu.SemaphoreType.DMA((len(sources),))],
        vmem=40 << 20,
    )
    keys = across_chips({0: marked}, loop_bits)
    states_sib = swap(states, "loop", 1)

    def route(m):
        return lambda block: block if m == 0 else swap(block, "groups", m)

    pool = lax.switch(partner_mask[0], [route(m) for m in range(group_size)], offered)

    qval, soft = call(
        hard_kernel,
        "hard",
        (shape((rows, rows), F32), shape((8, LANES), F32)),
        states,
        premises,
        pool,
        meta,
    )
    even = range(0, loop_size, 2)
    for m in even:
        if m:
            keys[m] = after(keys[m], soft)
    stats = call(
        functools.partial(early_kernel, len(even)),
        "early",
        shape((8, 2 * rows), F32),
        states,
        states_sib,
        soft,
        *(keys[m] for m in even),
    )
    stats_sib = swap(stats, "loop", 1)
    back = call(
        back_kernel, "back", shape((offer, width)), after(states, stats), qval, meta
    )
    stats_sib = after(stats_sib, back)
    lse, message = call(
        near_kernel,
        "near",
        (shape((8, 2 * rows), F32), shape((offer, width + LANES))),
        stats,
        stats_sib,
        back,
    )
    for m in even:
        keys[m] = after(keys[m], message)
    keys = from_sibling(keys)
    grad_states = call(
        functools.partial(states_kernel, loop_size),
        "states",
        shape((rows, width)),
        premises,
        *keys[1:],
        states,
        lse,
        pool,
        meta,
        qval,
        stats,
        stats_sib,
        cost=int(1.7e10),
    )
    for level in range(group_bits):
        last = level == group_bits - 1
        outs = (shape((offer, width)), shape((8, LANES), F32))
        if level == 1:
            grad, *far = call(
                functools.partial(premises_kernel, len(even)),
                "premises",
                (shape((rows, width), F32),) + (shape((rows, width)),) * (len(even) - 1),
                *(keys[m] for m in even),
                states,
                states_sib,
                after(lse, message),
                qval,
                stats,
                stats_sib,
                cost=int(1.7e10),
            )
        other = swap(message, "groups", 1 << level)
        if level == 2:
            other = after(other, grad_states)
        if level == 1:
            other = after(other, grad, *far)
            far = [
                swap(block, "loop", m)
                for m, block in zip(even[1:], far)
            ]
        message = call(
            functools.partial(merge_kernel, level, last),
            "merge",
            outs if last else shape(message.shape),
            message,
            other,
            meta,
        )
    home, part = message
    odd = lax.axis_index("loop") & 1

    def across(block):
        for bit in range(1, loop_bits):
            block = block + swap(block, "loop", 1 << bit)
        return block

    part = lax.cond(odd == 1, across, lambda block: block, part)
    grad_states, grad_premises = call(
        functools.partial(finish_kernel, len(far)),
        "finish",
        (shape((rows, width)), shape((rows, width))),
        grad_states,
        grad,
        home,
        meta,
        *far,
    )
    other = after(swap(part, "loop", 1), grad_premises)
    loss = call(
        functools.partial(loss_kernel, loop_size * group_size * rows),
        "loss",
        shape((1, 1), F32),
        part,
        other,
    )
    return loss[0, 0], grad_states, grad_premises


def solution(mesh):
    return jax.shard_map(
        body,
        mesh=mesh,
        in_specs=(
            P(("loop", "groups"), None),
            P(("loop", "groups"), None),
            P("loop", "groups"),
            P("loop"),
            P("loop", "groups", None),
            P(("loop", "groups")),
        ),
        out_specs=(P(), P(("loop", "groups"), None), P(("loop", "groups"), None)),
        check_vma=False,
    )
```

```python
import functools

import jax
import jax.numpy as jnp
from jax import lax
from jax.experimental import pallas as pl
from jax.experimental.pallas import tpu as pltpu
from jax.sharding import PartitionSpec as P

SCALE = 3.0
LANES = 128
F32 = jnp.float32
BF16 = jnp.bfloat16
VMEM = pl.BlockSpec(memory_space=pltpu.VMEM)
SMEM = pl.BlockSpec(memory_space=pltpu.SMEM)
HBM = pl.BlockSpec(memory_space=pltpu.HBM)


def swap(block, axis, mask):
    count = lax.axis_size(axis)
    return lax.ppermute(block, axis, [(i, i ^ mask) for i in range(count)])


def shape(dims, dtype=BF16):
    return jax.ShapeDtypeStruct(dims, dtype)


def call(kernel, name, outs, *args, ins=None, out_specs=None, scratch=(), cost=0, vmem=40 << 20):
    ins = ins or {}
    return pl.pallas_call(
        kernel,
        out_shape=outs,
        in_specs=[ins.get(i, VMEM) for i in range(len(args))],
        out_specs=out_specs or jax.tree.map(lambda _: VMEM, outs),
        scratch_shapes=scratch,
        compiler_params=pltpu.CompilerParams(vmem_limit_bytes=vmem),
        cost_estimate=pl.CostEstimate(flops=cost, bytes_accessed=0, transcendentals=0),
        name=name,
    )(*args)


def dot(a, b, dims):
    return lax.dot_general(a, b, (dims, ((), ())), preferred_element_type=F32)


def total(x):
    return jnp.sum(jnp.sum(x, axis=0, keepdims=True), axis=1, keepdims=True)


def parts(x):
    hi = x.astype(BF16)
    rest = x - hi.astype(F32)
    mid = rest.astype(BF16)
    low = (rest - mid.astype(F32)).astype(BF16)
    return hi, mid, low


def place_of(rows, picked):
    slot = lax.broadcasted_iota(jnp.int32, (rows, picked.shape[1]), 0)
    return jnp.where(slot == picked, 1.0, 0.0).astype(BF16)


def pick_of(offer, hard_idx):
    which = lax.broadcasted_iota(jnp.int32, (offer, hard_idx.shape[1]), 0)
    return jnp.where(which == hard_idx, 1.0, 0.0)


def column(rows):
    return lax.broadcasted_iota(jnp.int32, (rows, 1), 0).astype(F32)


def pack(message, block, scalar):
    offer, width = block.shape
    message[:, :width] = block.astype(BF16)
    row = lax.broadcasted_iota(jnp.int32, (offer, LANES), 0)
    hi, mid, low = (p.astype(F32) for p in parts(jnp.broadcast_to(scalar, row.shape)))
    spread = jnp.where(row == 0, hi, jnp.where(row == 1, mid, jnp.where(row == 2, low, 0.0)))
    message[:, width:] = spread.astype(BF16)


def unpack(message):
    width = message.shape[1] - LANES
    spread = message[:, width:].astype(F32)
    return message[:, :width], jnp.sum(spread, axis=0, keepdims=True)[:, 0:1]


def mark_kernel(premises, states, count, marked, both, held, sems):
    rows = premises.shape[0]
    copies = [
        pltpu.make_async_copy(premises, held, sems.at[0]),
        pltpu.make_async_copy(states, both.at[:rows, :], sems.at[1]),
    ]
    for copy in copies:
        copy.start()
    copies[0].wait()
    row = lax.broadcasted_iota(jnp.int32, (rows, LANES), 0)
    lane = lax.broadcasted_iota(jnp.int32, (rows, LANES), 1)
    invalid = jnp.logical_and(row >= count[0, 0], lane == 0)
    first = jnp.where(invalid, jnp.inf, held[:, :LANES].astype(F32)).astype(BF16)
    for target in (marked, both.at[rows:, :]):
        target[:, LANES:] = held[:, LANES:]
        target[:, :LANES] = first
    copies[1].wait()


def is_valid(key):
    return key[:, 0:1].astype(F32) < jnp.inf


def count_of(meta):
    return meta[3:4, 0:1].astype(F32)


def front_kernel(size, *refs):
    sources, (offered, meta), held = refs[:size], refs[size : size + 2], refs[size + 2 : -1]
    sems = refs[-1]
    copies = [
        pltpu.make_async_copy(source, target, sems.at[i])
        for i, (source, target) in enumerate(zip(sources, held))
    ]
    for copy in copies:
        copy.start()
    for copy in copies:
        copy.wait()
    premises, send_rows, hard_idx, mask, counts = held
    row = lax.broadcasted_iota(jnp.int32, meta.shape, 0)
    meta[...] = jnp.where(
        row == 0, hard_idx[...], jnp.where(row == 2, mask[...], counts[...])
    )
    meta[1:2, 0 : send_rows.shape[1]] = send_rows[...]
    place = place_of(premises.shape[0], send_rows[...])
    offered[...] = dot(place, premises[...], ((0,), (0,))).astype(BF16)


def back_kernel(states, qval, meta, back):
    offer = back.shape[0]
    weight = qval[:offer, :] * pick_of(offer, meta[0:1, :])
    split = jnp.concatenate(parts(weight), axis=0)
    summed = dot(split, states[...], ((1,), (0,)))
    summed = summed[:offer] + summed[offer : 2 * offer] + summed[2 * offer :]
    back[...] = (SCALE * summed).astype(BF16)


def line(width):
    return lax.broadcasted_iota(jnp.int32, (1, width), 1).astype(F32)


def mask_keys(scores, ok):
    return jnp.where(ok, scores, -jnp.inf)


def score(key, block, limit):
    return mask_keys(SCALE * dot(key, block, ((1,), (1,))), column(key.shape[0]) < limit)


def tops(blocks):
    return jnp.max(functools.reduce(jnp.maximum, blocks), axis=0, keepdims=True)


def masses(blocks, top):
    weights = functools.reduce(jnp.add, [jnp.exp(block - top) for block in blocks])
    return jnp.sum(weights, axis=0, keepdims=True)


def early_kernel(size, own, sib, pool, meta, *refs):
    keys, (stats, qval) = refs[:size], refs[size:]
    rows, offer = own.shape[0], pool.shape[0]
    both = jnp.concatenate([own[...], sib[:rows, :]], axis=0)
    oks = [is_valid(key) for key in keys]
    blocks = [SCALE * dot(key[...], both, ((1,), (1,))) for key in keys]
    slot = lax.broadcasted_iota(jnp.int32, (rows, rows), 0)
    mine = slot == lax.broadcasted_iota(jnp.int32, (rows, rows), 1)
    pos = jnp.sum(jnp.where(mine, blocks[0][:, :rows], 0.0), axis=0, keepdims=True)
    blocks = [mask_keys(block, ok) for block, ok in zip(blocks, oks)]
    top = tops(blocks)
    stats[0:1, :] = top
    stats[1:2, :] = masses(blocks, top)
    pick = pick_of(offer, meta[0:1, :])
    tval = SCALE * dot(pool[...], own[...], ((1,), (1,)))
    tval = jnp.sum(pick * tval, axis=0, keepdims=True)
    valid = line(rows) < count_of(meta)
    gap = tval - pos
    q = jnp.where(valid, 1.0 / (1.0 + jnp.exp(-gap)), 0.0)
    plus = jnp.maximum(gap, 0.0) + jnp.log(1.0 + jnp.exp(-jnp.abs(gap)))
    qval[...] = jnp.broadcast_to(q, qval.shape)
    info = jnp.broadcast_to(total(jnp.where(valid, plus - pos, 0.0)), (1, stats.shape[1]))
    for i, ok in enumerate(oks):
        info = jnp.where(line(stats.shape[1]) == 1 + i, total(jnp.where(ok, 1.0, 0.0)), info)
    stats[2:3, :] = info


def limit_of(stats, stats_sib, m):
    return (stats_sib if m & 1 else stats)[2:3, 1 + (m >> 1) : 2 + (m >> 1)]


def valid_lanes(stats, stats_sib, m, rows):
    slots = line(rows)
    pair = [slots < limit_of(stats, stats_sib, m + i) for i in range(2)]
    return jnp.concatenate(pair, axis=1)


def near_kernel(stats, stats_sib, back, lse, message):
    rows = stats.shape[1] // 2
    top, mass = stats[0:1, :], stats[1:2, :]
    flip = [
        jnp.concatenate([stats_sib[i : i + 1, rows:], stats_sib[i : i + 1, :rows]], axis=1)
        for i in range(2)
    ]
    best = jnp.maximum(top, flip[0])
    mass = mass * jnp.exp(top - best) + flip[1] * jnp.exp(flip[0] - best)
    out = best + jnp.log(mass)
    lse[...] = jnp.broadcast_to(out, lse.shape)
    out = jnp.where(valid_lanes(stats, stats_sib, 0, rows), out, 0.0)
    pack(message, back[...], total(out) + stats[2:3, 0:1] + stats_sib[2:3, 0:1])


def merge_kernel(level, last, mine, other, meta, *outs):
    block, scalar = unpack(mine)
    other_block, other_scalar = unpack(other)
    take = meta[2:3, 0:1] >> level & 1
    block = jnp.where(take == 1, other_block.astype(F32), block.astype(F32)).astype(BF16)
    scalar = scalar + other_scalar
    if last:
        outs[0][...] = block
        outs[1][...] = jnp.broadcast_to(scalar, outs[1].shape)
    else:
        pack(outs[0], block, scalar)


def states_kernel(size, *refs):
    keys = refs[:size]
    states, lse, pool, meta, qval, stats, stats_sib, out = refs[size:]
    rows, offer = states.shape[0], pool.shape[0]
    slot = column(rows)
    valid = slot < count_of(meta)
    limits = [limit_of(stats, stats_sib, m) for m in range(size)]
    cleared = [keys[0][...]] + [
        jnp.where(slot < limit, key[key.shape[0] - rows :, :].astype(F32), 0.0).astype(BF16)
        for key, limit in zip(keys[1:], limits[1:])
    ]
    cleared = jnp.concatenate(cleared, axis=0)
    scores = SCALE * dot(states[...], cleared, ((1,), (1,)))
    lse_column = jnp.broadcast_to(lse[0:1, :rows], (rows, rows)).T[:, 0:1]
    ok = jnp.concatenate([line(rows) < limit for limit in limits], axis=1)
    prob = jnp.where(jnp.logical_and(valid, ok), jnp.exp(scores - lse_column), 0.0)
    grad = dot(prob.astype(BF16), cleared, ((1,), (0,)))
    hard = dot(pick_of(offer, meta[0:1, :]).astype(BF16), pool[...], ((0,), (0,)))
    q = qval[...].T[:, 0:1]
    vq = jnp.where(valid, 1.0, 0.0) + q
    grad = grad + q * hard - vq * keys[0][...].astype(F32)
    out[...] = (SCALE * grad).astype(BF16)


def premises_kernel(size, *refs):
    keys = refs[:size]
    own, sib, lse, qval, stats, stats_sib, near = refs[size : size + 7]
    far = refs[size + 7 :]
    rows = own.shape[0]
    both = jnp.concatenate([own[...], sib[:rows, :]], axis=0)
    row_ok = valid_lanes(stats, stats_sib, 0, rows)
    held = jnp.concatenate([key[...] for key in keys], axis=0)
    scores = SCALE * dot(held, both, ((1,), (1,)))
    ok = jnp.logical_and(is_valid(held), row_ok)
    prob = jnp.where(ok, jnp.exp(scores - lse[0:1, :]), 0.0).astype(BF16)
    grad = dot(prob, both, ((1,), (0,)))
    vq = jnp.where(is_valid(keys[0]), 1.0, 0.0) + qval[...].T[:, 0:1]
    near[...] = grad[:rows] - SCALE * vq * own[...].astype(F32)
    for i, out in enumerate(far):
        out[...] = grad[(i + 1) * rows : (i + 2) * rows].astype(BF16)


def finish_kernel(size, grad_states, grad, home, meta, *refs):
    far, (out_states, out) = refs[:size], refs[size:]
    place = place_of(grad.shape[0], meta[1:2, 0 : home.shape[0]])
    summed = grad[...] + dot(place, home[...], ((1,), (0,)))
    for block in far:
        summed = summed + block[...].astype(F32)
    out[...] = summed.astype(BF16)
    out_states[...] = grad_states[...]


def loss_kernel(count, part, other, out):
    odd = jnp.full((1, 1), lax.axis_index("loop") & 1, jnp.int32) == 1
    out[...] = jnp.where(odd, part[0:1, 0:1], other[0:1, 0:1]) / count


def across_chips(held, bits):
    for bit in reversed(range(1, bits)):
        held.update({m | 1 << bit: swap(b, "loop", 1 << bit) for m, b in held.items()})
    return held


def from_sibling(held):
    for m in [m for m in held if not m & 1 and m | 1 not in held]:
        held[m | 1] = swap(held[m], "loop", 1)
    return [held[m] for m in range(len(held))]


def body(states, premises, counts, partner_mask, send_rows, hard_idx):
    rows, width = states.shape
    offer = send_rows.shape[2]
    loop_size = lax.axis_size("loop")
    group_size = lax.axis_size("groups")
    loop_bits = loop_size.bit_length() - 1
    group_bits = group_size.bit_length() - 1

    def after(value, *earlier):
        return lax.optimization_barrier((value, *earlier))[0] if earlier else value

    sources = (premises, send_rows[0], hard_idx[None, :], partner_mask[None, :], counts)
    marked, both = call(
        mark_kernel,
        "mark",
        (shape((rows, width)), shape((2 * rows, width))),
        premises,
        states,
        counts,
        ins={0: HBM, 1: HBM, 2: SMEM},
        scratch=[pltpu.VMEM((rows, width), BF16), pltpu.SemaphoreType.DMA((2,))],
    )
    offered, meta = call(
        functools.partial(front_kernel, len(sources)),
        "front",
        (shape((offer, width)), shape((8, rows), jnp.int32)),
        *sources,
        ins={i: HBM for i in range(len(sources))},
        scratch=[pltpu.VMEM(source.shape, source.dtype) for source in sources]
        + [pltpu.SemaphoreType.DMA((len(sources),))],
        vmem=40 << 20,
    )
    keys = across_chips({0: marked}, loop_bits)
    both_sib = swap(both, "loop", 1)

    def route(m):
        return lambda block: block if m == 0 else swap(block, "groups", m)

    pool = lax.switch(partner_mask[0], [route(m) for m in range(group_size)], offered)

    even = range(0, loop_size, 2)
    forward = dict(keys)
    for m in even:
        if m:
            keys[m] = after(keys[m], pool)
    stats, qval = call(
        functools.partial(early_kernel, len(even)),
        "early",
        (shape((8, 2 * rows), F32), shape((rows, rows), F32)),
        states,
        both_sib,
        pool,
        meta,
        *(keys[m] for m in even),
    )
    stats_sib = swap(stats, "loop", 1)
    back = call(
        back_kernel, "back", shape((offer, width)), after(states, stats), qval, meta
    )
    stats_sib = after(stats_sib, back)
    lse, message = call(
        near_kernel,
        "near",
        (shape((8, 2 * rows), F32), shape((offer, width + LANES))),
        stats,
        stats_sib,
        back,
    )
    held = [keys[m] for m in even]
    for m in even[1:]:
        keys[m | 1] = swap(after(forward[m], pool), "loop", 1)
    keys[1] = both_sib
    keys = [keys[m] for m in range(loop_size)]

    def states_part():
        return call(
            functools.partial(states_kernel, loop_size),
            "states",
            shape((rows, width)),
            premises,
            *keys[1:],
            states,
            lse,
            pool,
            meta,
            qval,
            stats,
            stats_sib,
            cost=int(1.7e10),
        )

    def premises_part(lse):
        grad, *far = call(
            functools.partial(premises_kernel, len(even)),
            "premises",
            (shape((rows, width), F32),) + (shape((rows, width)),) * (len(even) - 1),
            *held,
            states,
            both_sib,
            lse,
            qval,
            stats,
            stats_sib,
            cost=int(1.7e10),
        )
        return grad, far

    def send(far):
        return [swap(block, "loop", m) for m, block in zip(even[1:], far)]

    def finish(grad_states, grad, home, sent):
        return call(
            functools.partial(finish_kernel, len(sent)),
            "finish",
            (shape((rows, width)), shape((rows, width))),
            grad_states,
            grad,
            home,
            meta,
            *sent,
        )

    def odd_core():
        held = message
        for level in range(group_bits):
            last = level == group_bits - 1
            if level == 0:
                grad, far = premises_part(after(lse, held))
            other = swap(held, "groups", 1 << level)
            if level == 0:
                other = after(other, grad, *far)
                sent = send(far)
            if level == 1:
                grad_states = states_part()
                other = after(other, grad_states)
            held = call(
                functools.partial(merge_kernel, level, last),
                "merge",
                (shape((offer, width)), shape((8, LANES), F32)) if last else shape(held.shape),
                held,
                other,
                meta,
            )
        home, part = held
        grads = finish(grad_states, grad, home, sent)
        for bit in range(1, loop_bits):
            other = swap(part, "loop", 1 << bit)
            part = part + (after(other, *grads) if bit == 1 else other)
        return part, *grads

    def even_core():
        grad, far = premises_part(lse)
        sent = send(far)
        home = lax.switch(
            partner_mask[0], [route(m) for m in range(group_size)], after(back, grad)
        )
        return jnp.zeros((8, LANES), F32), *finish(states_part(), grad, home, sent)

    odd = lax.axis_index("loop") & 1
    part, grad_states, grad_premises = lax.cond(odd == 1, odd_core, even_core)
    loss = call(
        functools.partial(loss_kernel, loop_size * group_size * rows),
        "loss",
        shape((1, 1), F32),
        part,
        swap(part, "loop", 1),
    )
    return loss[0, 0], grad_states, grad_premises


def solution(mesh):
    return jax.shard_map(
        body,
        mesh=mesh,
        in_specs=(
            P(("loop", "groups"), None),
            P(("loop", "groups"), None),
            P("loop", "groups"),
            P("loop"),
            P("loop", "groups", None),
            P(("loop", "groups")),
        ),
        out_specs=(P(), P(("loop", "groups"), None), P(("loop", "groups"), None)),
        check_vma=False,
    )
```

```python
import functools

import jax
import jax.numpy as jnp
from jax import lax
from jax.experimental import pallas as pl
from jax.experimental.pallas import tpu as pltpu
from jax.sharding import PartitionSpec as P

SCALE = 3.0
LANES = 128
F32 = jnp.float32
BF16 = jnp.bfloat16
VMEM = pl.BlockSpec(memory_space=pltpu.VMEM)
SMEM = pl.BlockSpec(memory_space=pltpu.SMEM)
HBM = pl.BlockSpec(memory_space=pltpu.HBM)


def swap(block, axis, mask):
    count = lax.axis_size(axis)
    return lax.ppermute(block, axis, [(i, i ^ mask) for i in range(count)])


def shape(dims, dtype=BF16):
    return jax.ShapeDtypeStruct(dims, dtype)


def call(kernel, name, outs, *args, ins=None, out_specs=None, scratch=(), cost=0, vmem=40 << 20):
    ins = ins or {}
    return pl.pallas_call(
        kernel,
        out_shape=outs,
        in_specs=[ins.get(i, VMEM) for i in range(len(args))],
        out_specs=out_specs or jax.tree.map(lambda _: VMEM, outs),
        scratch_shapes=scratch,
        compiler_params=pltpu.CompilerParams(vmem_limit_bytes=vmem),
        cost_estimate=pl.CostEstimate(flops=cost, bytes_accessed=0, transcendentals=0),
        name=name,
    )(*args)


def dot(a, b, dims):
    return lax.dot_general(a, b, (dims, ((), ())), preferred_element_type=F32)


def total(x):
    return jnp.sum(jnp.sum(x, axis=0, keepdims=True), axis=1, keepdims=True)


def parts(x):
    hi = x.astype(BF16)
    rest = x - hi.astype(F32)
    mid = rest.astype(BF16)
    low = (rest - mid.astype(F32)).astype(BF16)
    return hi, mid, low


def place_of(rows, picked):
    slot = lax.broadcasted_iota(jnp.int32, (rows, picked.shape[1]), 0)
    return jnp.where(slot == picked, 1.0, 0.0).astype(BF16)


def pick_of(offer, hard_idx):
    which = lax.broadcasted_iota(jnp.int32, (offer, hard_idx.shape[1]), 0)
    return jnp.where(which == hard_idx, 1.0, 0.0)


def column(rows):
    return lax.broadcasted_iota(jnp.int32, (rows, 1), 0).astype(F32)


def pack(message, block, scalar):
    offer, width = block.shape
    message[:, :width] = block.astype(BF16)
    row = lax.broadcasted_iota(jnp.int32, (offer, LANES), 0)
    hi, mid, low = (p.astype(F32) for p in parts(jnp.broadcast_to(scalar, row.shape)))
    spread = jnp.where(row == 0, hi, jnp.where(row == 1, mid, jnp.where(row == 2, low, 0.0)))
    message[:, width:] = spread.astype(BF16)


def unpack(message):
    width = message.shape[1] - LANES
    spread = message[:, width:].astype(F32)
    return message[:, :width], jnp.sum(spread, axis=0, keepdims=True)[:, 0:1]


def mark_kernel(premises, count, marked, sems):
    rows = premises.shape[0]
    size = rows // 1
    pieces = [pl.ds(i * size, size) for i in range(1)]
    copies = [
        pltpu.make_async_copy(premises.at[piece, :], marked.at[piece, :], sems.at[i])
        for i, piece in enumerate(pieces)
    ]
    for copy in copies:
        copy.start()
    for i, copy in enumerate(copies):
        copy.wait()
        row = lax.broadcasted_iota(jnp.int32, (size, LANES), 0) + i * size
        lane = lax.broadcasted_iota(jnp.int32, (size, LANES), 1)
        invalid = jnp.logical_and(row >= count[0, 0], lane == 0)
        first = marked[pieces[i], :LANES].astype(F32)
        marked[pieces[i], :LANES] = jnp.where(invalid, jnp.inf, first).astype(BF16)


def is_valid(key):
    return key[:, 0:1].astype(F32) < jnp.inf


def count_of(meta):
    return meta[3:4, 0:1].astype(F32)


def front_kernel(size, *refs):
    sources, (offered, meta), held = refs[:size], refs[size : size + 2], refs[size + 2 : -1]
    sems = refs[-1]
    copies = [
        pltpu.make_async_copy(source, target, sems.at[i])
        for i, (source, target) in enumerate(zip(sources, held))
    ]
    for copy in copies:
        copy.start()
    for copy in copies:
        copy.wait()
    premises, send_rows, hard_idx, mask, counts = held
    row = lax.broadcasted_iota(jnp.int32, meta.shape, 0)
    meta[...] = jnp.where(
        row == 0, hard_idx[...], jnp.where(row == 2, mask[...], counts[...])
    )
    meta[1:2, 0 : send_rows.shape[1]] = send_rows[...]
    place = place_of(premises.shape[0], send_rows[...])
    offered[...] = dot(place, premises[...], ((0,), (0,))).astype(BF16)


def back_kernel(states, qval, meta, back):
    offer = back.shape[0]
    weight = qval[:offer, :] * pick_of(offer, meta[0:1, :])
    split = jnp.concatenate(parts(weight), axis=0)
    summed = dot(split, states[...], ((1,), (0,)))
    summed = summed[:offer] + summed[offer : 2 * offer] + summed[2 * offer :]
    back[...] = (SCALE * summed).astype(BF16)


def line(width):
    return lax.broadcasted_iota(jnp.int32, (1, width), 1).astype(F32)


def mask_keys(scores, ok):
    return jnp.where(ok, scores, -jnp.inf)


def score(key, block, limit):
    return mask_keys(SCALE * dot(key, block, ((1,), (1,))), column(key.shape[0]) < limit)


def tops(blocks):
    return jnp.max(functools.reduce(jnp.maximum, blocks), axis=0, keepdims=True)


def masses(blocks, top):
    weights = functools.reduce(jnp.add, [jnp.exp(block - top) for block in blocks])
    return jnp.sum(weights, axis=0, keepdims=True)


def early_kernel(size, own, sib, pool, meta, *refs):
    keys, (stats, qval) = refs[:size], refs[size:]
    rows, offer = own.shape[0], pool.shape[0]
    both = jnp.concatenate([own[...], sib[...]], axis=0)
    oks = [is_valid(key) for key in keys]
    blocks = [SCALE * dot(key[...], both, ((1,), (1,))) for key in keys]
    slot = lax.broadcasted_iota(jnp.int32, (rows, rows), 0)
    mine = slot == lax.broadcasted_iota(jnp.int32, (rows, rows), 1)
    pos = jnp.sum(jnp.where(mine, blocks[0][:, :rows], 0.0), axis=0, keepdims=True)
    blocks = [mask_keys(block, ok) for block, ok in zip(blocks, oks)]
    top = tops(blocks)
    stats[0:1, :] = top
    stats[1:2, :] = masses(blocks, top)
    pick = pick_of(offer, meta[0:1, :])
    tval = SCALE * dot(pool[...], own[...], ((1,), (1,)))
    tval = jnp.sum(pick * tval, axis=0, keepdims=True)
    valid = line(rows) < count_of(meta)
    gap = tval - pos
    q = jnp.where(valid, 1.0 / (1.0 + jnp.exp(-gap)), 0.0)
    plus = jnp.maximum(gap, 0.0) + jnp.log(1.0 + jnp.exp(-jnp.abs(gap)))
    qval[...] = jnp.broadcast_to(q, qval.shape)
    info = jnp.broadcast_to(total(jnp.where(valid, plus - pos, 0.0)), (1, stats.shape[1]))
    for i, ok in enumerate(oks):
        info = jnp.where(line(stats.shape[1]) == 1 + i, total(jnp.where(ok, 1.0, 0.0)), info)
    stats[2:3, :] = info


def limit_of(stats, stats_sib, m):
    return (stats_sib if m & 1 else stats)[2:3, 1 + (m >> 1) : 2 + (m >> 1)]


def valid_lanes(stats, stats_sib, m, rows):
    slots = line(rows)
    pair = [slots < limit_of(stats, stats_sib, m + i) for i in range(2)]
    return jnp.concatenate(pair, axis=1)


def near_kernel(stats, stats_sib, back, lse, message):
    rows = stats.shape[1] // 2
    top, mass = stats[0:1, :], stats[1:2, :]
    flip = [
        jnp.concatenate([stats_sib[i : i + 1, rows:], stats_sib[i : i + 1, :rows]], axis=1)
        for i in range(2)
    ]
    best = jnp.maximum(top, flip[0])
    mass = mass * jnp.exp(top - best) + flip[1] * jnp.exp(flip[0] - best)
    out = best + jnp.log(mass)
    lse[...] = jnp.broadcast_to(out, lse.shape)
    out = jnp.where(valid_lanes(stats, stats_sib, 0, rows), out, 0.0)
    pack(message, back[...], total(out) + stats[2:3, 0:1] + stats_sib[2:3, 0:1])


def merge_kernel(level, last, mine, other, meta, *outs):
    block, scalar = unpack(mine)
    other_block, other_scalar = unpack(other)
    take = meta[2:3, 0:1] >> level & 1
    block = jnp.where(take == 1, other_block.astype(F32), block.astype(F32)).astype(BF16)
    scalar = scalar + other_scalar
    if last:
        outs[0][...] = block
        outs[1][...] = jnp.broadcast_to(scalar, outs[1].shape)
    else:
        pack(outs[0], block, scalar)


def states_kernel(size, *refs):
    keys = refs[:size]
    states, lse, pool, meta, qval, stats, stats_sib, out = refs[size:]
    rows, offer = states.shape[0], pool.shape[0]
    slot = column(rows)
    valid = slot < count_of(meta)
    limits = [limit_of(stats, stats_sib, m) for m in range(size)]
    cleared = [keys[0][...]] + [
        jnp.where(slot < limit, key[...].astype(F32), 0.0).astype(BF16)
        for key, limit in zip(keys[1:], limits[1:])
    ]
    cleared = jnp.concatenate(cleared, axis=0)
    scores = SCALE * dot(states[...], cleared, ((1,), (1,)))
    lse_column = jnp.broadcast_to(lse[0:1, :rows], (rows, rows)).T[:, 0:1]
    ok = jnp.concatenate([line(rows) < limit for limit in limits], axis=1)
    prob = jnp.where(jnp.logical_and(valid, ok), jnp.exp(scores - lse_column), 0.0)
    grad = dot(prob.astype(BF16), cleared, ((1,), (0,)))
    hard = dot(pick_of(offer, meta[0:1, :]).astype(BF16), pool[...], ((0,), (0,)))
    q = qval[...].T[:, 0:1]
    vq = jnp.where(valid, 1.0, 0.0) + q
    grad = grad + q * hard - vq * keys[0][...].astype(F32)
    out[...] = (SCALE * grad).astype(BF16)


def premises_kernel(size, *refs):
    keys = refs[:size]
    own, sib, lse, qval, stats, stats_sib, near = refs[size : size + 7]
    far = refs[size + 7 :]
    rows = own.shape[0]
    both = jnp.concatenate([own[...], sib[...]], axis=0)
    row_ok = valid_lanes(stats, stats_sib, 0, rows)
    held = jnp.concatenate([key[...] for key in keys], axis=0)
    scores = SCALE * dot(held, both, ((1,), (1,)))
    ok = jnp.logical_and(is_valid(held), row_ok)
    prob = jnp.where(ok, jnp.exp(scores - lse[0:1, :]), 0.0).astype(BF16)
    grad = dot(prob, both, ((1,), (0,)))
    vq = jnp.where(is_valid(keys[0]), 1.0, 0.0) + qval[...].T[:, 0:1]
    near[...] = grad[:rows] - SCALE * vq * own[...].astype(F32)
    for i, out in enumerate(far):
        out[...] = grad[(i + 1) * rows : (i + 2) * rows].astype(BF16)


def finish_kernel(size, grad_states, grad, home, meta, *refs):
    far, (out_states, out) = refs[:size], refs[size:]
    place = place_of(grad.shape[0], meta[1:2, 0 : home.shape[0]])
    summed = grad[...] + dot(place, home[...], ((1,), (0,)))
    for block in far:
        summed = summed + block[...].astype(F32)
    out[...] = summed.astype(BF16)
    out_states[...] = grad_states[...]


def loss_kernel(count, part, other, out):
    odd = jnp.full((1, 1), lax.axis_index("loop") & 1, jnp.int32) == 1
    out[...] = jnp.where(odd, part[0:1, 0:1], other[0:1, 0:1]) / count


def across_chips(held, bits):
    for bit in reversed(range(1, bits)):
        held.update({m | 1 << bit: swap(b, "loop", 1 << bit) for m, b in held.items()})
    return held


def from_sibling(held):
    for m in [m for m in held if not m & 1 and m | 1 not in held]:
        held[m | 1] = swap(held[m], "loop", 1)
    return [held[m] for m in range(len(held))]


def body(states, premises, counts, partner_mask, send_rows, hard_idx):
    rows, width = states.shape
    offer = send_rows.shape[2]
    loop_size = lax.axis_size("loop")
    group_size = lax.axis_size("groups")
    loop_bits = loop_size.bit_length() - 1
    group_bits = group_size.bit_length() - 1

    def after(value, *earlier):
        return lax.optimization_barrier((value, *earlier))[0] if earlier else value

    sources = (premises, send_rows[0], hard_idx[None, :], partner_mask[None, :], counts)
    marked = call(
        mark_kernel,
        "mark",
        shape((rows, width)),
        premises,
        counts,
        ins={0: HBM, 1: SMEM},
        scratch=[pltpu.SemaphoreType.DMA((1,))],
        vmem=40 << 20,
    )
    offered, meta = call(
        functools.partial(front_kernel, len(sources)),
        "front",
        (shape((offer, width)), shape((8, rows), jnp.int32)),
        *sources,
        ins={i: HBM for i in range(len(sources))},
        scratch=[pltpu.VMEM(source.shape, source.dtype) for source in sources]
        + [pltpu.SemaphoreType.DMA((len(sources),))],
        vmem=40 << 20,
    )
    keys = across_chips({0: marked}, loop_bits)
    states_sib = swap(states, "loop", 1)

    def route(m):
        return lambda block: block if m == 0 else swap(block, "groups", m)

    pool = lax.switch(partner_mask[0], [route(m) for m in range(group_size)], offered)

    even = range(0, loop_size, 2)
    forward = dict(keys)
    for m in even:
        if m:
            keys[m] = after(keys[m], pool)
    stats, qval = call(
        functools.partial(early_kernel, len(even)),
        "early",
        (shape((8, 2 * rows), F32), shape((rows, rows), F32)),
        states,
        states_sib,
        pool,
        meta,
        *(keys[m] for m in even),
    )
    stats_sib = swap(stats, "loop", 1)
    back = call(
        back_kernel, "back", shape((offer, width)), after(states, stats), qval, meta
    )
    stats_sib = after(stats_sib, back)
    lse, message = call(
        near_kernel,
        "near",
        (shape((8, 2 * rows), F32), shape((offer, width + LANES))),
        stats,
        stats_sib,
        back,
    )
    held = [keys[m] for m in even]
    for m in even:
        keys[m | 1] = swap(after(forward[m], pool), "loop", 1)
    keys = [keys[m] for m in range(loop_size)]

    def states_part():
        return call(
            functools.partial(states_kernel, loop_size),
            "states",
            shape((rows, width)),
            premises,
            *keys[1:],
            states,
            lse,
            pool,
            meta,
            qval,
            stats,
            stats_sib,
            cost=int(1.7e10),
        )

    def premises_part(lse):
        grad, *far = call(
            functools.partial(premises_kernel, len(even)),
            "premises",
            (shape((rows, width), F32),) + (shape((rows, width)),) * (len(even) - 1),
            *held,
            states,
            states_sib,
            lse,
            qval,
            stats,
            stats_sib,
            cost=int(1.7e10),
        )
        return grad, far

    def send(far):
        return [swap(block, "loop", m) for m, block in zip(even[1:], far)]

    def finish(grad_states, grad, home, sent):
        return call(
            functools.partial(finish_kernel, len(sent)),
            "finish",
            (shape((rows, width)), shape((rows, width))),
            grad_states,
            grad,
            home,
            meta,
            *sent,
        )

    def odd_core():
        held = message
        for level in range(group_bits):
            last = level == group_bits - 1
            if level == 0:
                grad, far = premises_part(after(lse, held))
            other = swap(held, "groups", 1 << level)
            if level == 0:
                other = after(other, grad, *far)
                sent = send(far)
            if level == 2:
                grad_states = states_part()
                other = after(other, grad_states)
            held = call(
                functools.partial(merge_kernel, level, last),
                "merge",
                (shape((offer, width)), shape((8, LANES), F32)) if last else shape(held.shape),
                held,
                other,
                meta,
            )
        home, part = held
        grads = finish(grad_states, grad, home, sent)
        for bit in range(1, loop_bits):
            other = swap(part, "loop", 1 << bit)
            part = part + (after(other, *grads) if bit == 1 else other)
        return part, *grads

    def even_core():
        grad, far = premises_part(lse)
        sent = send(far)
        home = lax.switch(
            partner_mask[0], [route(m) for m in range(group_size)], after(back, grad)
        )
        return jnp.zeros((8, LANES), F32), *finish(states_part(), grad, home, sent)

    odd = lax.axis_index("loop") & 1
    part, grad_states, grad_premises = lax.cond(odd == 1, odd_core, even_core)
    loss = call(
        functools.partial(loss_kernel, loop_size * group_size * rows),
        "loss",
        shape((1, 1), F32),
        part,
        swap(part, "loop", 1),
    )
    return loss[0, 0], grad_states, grad_premises


def solution(mesh):
    return jax.shard_map(
        body,
        mesh=mesh,
        in_specs=(
            P(("loop", "groups"), None),
            P(("loop", "groups"), None),
            P("loop", "groups"),
            P("loop"),
            P("loop", "groups", None),
            P(("loop", "groups")),
        ),
        out_specs=(P(), P(("loop", "groups"), None), P(("loop", "groups"), None)),
        check_vma=False,
    )
```

```python
import functools

import jax
import jax.numpy as jnp
from jax import lax
from jax.experimental import pallas as pl
from jax.experimental.pallas import tpu as pltpu
from jax.sharding import PartitionSpec as P

SCALE = 3.0
LANES = 128
F32 = jnp.float32
BF16 = jnp.bfloat16
VMEM = pl.BlockSpec(memory_space=pltpu.VMEM)
SMEM = pl.BlockSpec(memory_space=pltpu.SMEM)
HBM = pl.BlockSpec(memory_space=pltpu.HBM)


def swap(block, axis, mask):
    count = lax.axis_size(axis)
    return lax.ppermute(block, axis, [(i, i ^ mask) for i in range(count)])


def shape(dims, dtype=BF16):
    return jax.ShapeDtypeStruct(dims, dtype)


def call(kernel, name, outs, *args, ins=None, out_specs=None, scratch=(), cost=0, vmem=40 << 20):
    ins = ins or {}
    return pl.pallas_call(
        kernel,
        out_shape=outs,
        in_specs=[ins.get(i, VMEM) for i in range(len(args))],
        out_specs=out_specs or jax.tree.map(lambda _: VMEM, outs),
        scratch_shapes=scratch,
        compiler_params=pltpu.CompilerParams(vmem_limit_bytes=vmem),
        cost_estimate=pl.CostEstimate(flops=cost, bytes_accessed=0, transcendentals=0),
        name=name,
    )(*args)


def dot(a, b, dims):
    return lax.dot_general(a, b, (dims, ((), ())), preferred_element_type=F32)


def total(x):
    return jnp.sum(jnp.sum(x, axis=0, keepdims=True), axis=1, keepdims=True)


def parts(x):
    hi = x.astype(BF16)
    rest = x - hi.astype(F32)
    mid = rest.astype(BF16)
    low = (rest - mid.astype(F32)).astype(BF16)
    return hi, mid, low


def place_of(rows, picked):
    slot = lax.broadcasted_iota(jnp.int32, (rows, picked.shape[1]), 0)
    return jnp.where(slot == picked, 1.0, 0.0).astype(BF16)


def pick_of(offer, hard_idx):
    which = lax.broadcasted_iota(jnp.int32, (offer, hard_idx.shape[1]), 0)
    return jnp.where(which == hard_idx, 1.0, 0.0)


def column(rows):
    return lax.broadcasted_iota(jnp.int32, (rows, 1), 0).astype(F32)


def pack(message, block, scalar):
    offer, width = block.shape
    message[:, :width] = block.astype(BF16)
    row = lax.broadcasted_iota(jnp.int32, (offer, LANES), 0)
    hi, mid, low = (p.astype(F32) for p in parts(jnp.broadcast_to(scalar, row.shape)))
    spread = jnp.where(row == 0, hi, jnp.where(row == 1, mid, jnp.where(row == 2, low, 0.0)))
    message[:, width:] = spread.astype(BF16)


def unpack(message):
    width = message.shape[1] - LANES
    spread = message[:, width:].astype(F32)
    return message[:, :width], jnp.sum(spread, axis=0, keepdims=True)[:, 0:1]


def mark_kernel(premises, count, marked, sems):
    rows = premises.shape[0]
    size = rows // 1
    pieces = [pl.ds(i * size, size) for i in range(1)]
    copies = [
        pltpu.make_async_copy(premises.at[piece, :], marked.at[piece, :], sems.at[i])
        for i, piece in enumerate(pieces)
    ]
    for copy in copies:
        copy.start()
    for i, copy in enumerate(copies):
        copy.wait()
        row = lax.broadcasted_iota(jnp.int32, (size, LANES), 0) + i * size
        lane = lax.broadcasted_iota(jnp.int32, (size, LANES), 1)
        invalid = jnp.logical_and(row >= count[0, 0], lane == 0)
        first = marked[pieces[i], :LANES].astype(F32)
        marked[pieces[i], :LANES] = jnp.where(invalid, jnp.inf, first).astype(BF16)


def pair_kernel(states, marked, both):
    rows = states.shape[0]
    both[:rows, :] = states[...]
    both[rows:, :] = marked[...]


def is_valid(key):
    return key[:, 0:1].astype(F32) < jnp.inf


def count_of(meta):
    return meta[3:4, 0:1].astype(F32)


def front_kernel(size, *refs):
    sources, (offered, meta), held = refs[:size], refs[size : size + 2], refs[size + 2 : -1]
    sems = refs[-1]
    copies = [
        pltpu.make_async_copy(source, target, sems.at[i])
        for i, (source, target) in enumerate(zip(sources, held))
    ]
    for copy in copies:
        copy.start()
    for copy in copies:
        copy.wait()
    premises, send_rows, hard_idx, mask, counts = held
    row = lax.broadcasted_iota(jnp.int32, meta.shape, 0)
    meta[...] = jnp.where(
        row == 0, hard_idx[...], jnp.where(row == 2, mask[...], counts[...])
    )
    meta[1:2, 0 : send_rows.shape[1]] = send_rows[...]
    place = place_of(premises.shape[0], send_rows[...])
    offered[...] = dot(place, premises[...], ((0,), (0,))).astype(BF16)


def back_kernel(states, qval, meta, back):
    offer = back.shape[0]
    weight = qval[:offer, :] * pick_of(offer, meta[0:1, :])
    split = jnp.concatenate(parts(weight), axis=0)
    summed = dot(split, states[...], ((1,), (0,)))
    summed = summed[:offer] + summed[offer : 2 * offer] + summed[2 * offer :]
    back[...] = (SCALE * summed).astype(BF16)


def line(width):
    return lax.broadcasted_iota(jnp.int32, (1, width), 1).astype(F32)


def mask_keys(scores, ok):
    return jnp.where(ok, scores, -jnp.inf)


def score(key, block, limit):
    return mask_keys(SCALE * dot(key, block, ((1,), (1,))), column(key.shape[0]) < limit)


def tops(blocks):
    return jnp.max(functools.reduce(jnp.maximum, blocks), axis=0, keepdims=True)


def masses(blocks, top):
    weights = functools.reduce(jnp.add, [jnp.exp(block - top) for block in blocks])
    return jnp.sum(weights, axis=0, keepdims=True)


def early_kernel(size, own, sib, pool, meta, *refs):
    keys, (stats, qval) = refs[:size], refs[size:]
    rows, offer = own.shape[0], pool.shape[0]
    both = jnp.concatenate([own[...], sib[: own.shape[0], :]], axis=0)
    oks = [is_valid(key) for key in keys]
    blocks = [SCALE * dot(key[...], both, ((1,), (1,))) for key in keys]
    slot = lax.broadcasted_iota(jnp.int32, (rows, rows), 0)
    mine = slot == lax.broadcasted_iota(jnp.int32, (rows, rows), 1)
    pos = jnp.sum(jnp.where(mine, blocks[0][:, :rows], 0.0), axis=0, keepdims=True)
    blocks = [mask_keys(block, ok) for block, ok in zip(blocks, oks)]
    top = tops(blocks)
    stats[0:1, :] = top
    stats[1:2, :] = masses(blocks, top)
    pick = pick_of(offer, meta[0:1, :])
    tval = SCALE * dot(pool[...], own[...], ((1,), (1,)))
    tval = jnp.sum(pick * tval, axis=0, keepdims=True)
    valid = line(rows) < count_of(meta)
    gap = tval - pos
    q = jnp.where(valid, 1.0 / (1.0 + jnp.exp(-gap)), 0.0)
    plus = jnp.maximum(gap, 0.0) + jnp.log(1.0 + jnp.exp(-jnp.abs(gap)))
    qval[...] = jnp.broadcast_to(q, qval.shape)
    info = jnp.broadcast_to(total(jnp.where(valid, plus - pos, 0.0)), (1, stats.shape[1]))
    for i, ok in enumerate(oks):
        info = jnp.where(line(stats.shape[1]) == 1 + i, total(jnp.where(ok, 1.0, 0.0)), info)
    stats[2:3, :] = info


def limit_of(stats, stats_sib, m):
    return (stats_sib if m & 1 else stats)[2:3, 1 + (m >> 1) : 2 + (m >> 1)]


def valid_lanes(stats, stats_sib, m, rows):
    slots = line(rows)
    pair = [slots < limit_of(stats, stats_sib, m + i) for i in range(2)]
    return jnp.concatenate(pair, axis=1)


def near_kernel(stats, stats_sib, back, lse, message):
    rows = stats.shape[1] // 2
    top, mass = stats[0:1, :], stats[1:2, :]
    flip = [
        jnp.concatenate([stats_sib[i : i + 1, rows:], stats_sib[i : i + 1, :rows]], axis=1)
        for i in range(2)
    ]
    best = jnp.maximum(top, flip[0])
    mass = mass * jnp.exp(top - best) + flip[1] * jnp.exp(flip[0] - best)
    out = best + jnp.log(mass)
    lse[...] = jnp.broadcast_to(out, lse.shape)
    out = jnp.where(valid_lanes(stats, stats_sib, 0, rows), out, 0.0)
    pack(message, back[...], total(out) + stats[2:3, 0:1] + stats_sib[2:3, 0:1])


def merge_kernel(level, last, mine, other, meta, *outs):
    block, scalar = unpack(mine)
    other_block, other_scalar = unpack(other)
    take = meta[2:3, 0:1] >> level & 1
    block = jnp.where(take == 1, other_block.astype(F32), block.astype(F32)).astype(BF16)
    scalar = scalar + other_scalar
    if last:
        outs[0][...] = block
        outs[1][...] = jnp.broadcast_to(scalar, outs[1].shape)
    else:
        pack(outs[0], block, scalar)


def states_kernel(size, *refs):
    keys = refs[:size]
    states, lse, pool, meta, qval, stats, stats_sib, out = refs[size:]
    rows, offer = states.shape[0], pool.shape[0]
    slot = column(rows)
    valid = slot < count_of(meta)
    limits = [limit_of(stats, stats_sib, m) for m in range(size)]
    cleared = [keys[0][...]] + [
        jnp.where(slot < limit, key[key.shape[0] - rows :, :].astype(F32), 0.0).astype(BF16)
        for key, limit in zip(keys[1:], limits[1:])
    ]
    cleared = jnp.concatenate(cleared, axis=0)
    scores = SCALE * dot(states[...], cleared, ((1,), (1,)))
    lse_column = jnp.broadcast_to(lse[0:1, :rows], (rows, rows)).T[:, 0:1]
    ok = jnp.concatenate([line(rows) < limit for limit in limits], axis=1)
    prob = jnp.where(jnp.logical_and(valid, ok), jnp.exp(scores - lse_column), 0.0)
    grad = dot(prob.astype(BF16), cleared, ((1,), (0,)))
    hard = dot(pick_of(offer, meta[0:1, :]).astype(BF16), pool[...], ((0,), (0,)))
    q = qval[...].T[:, 0:1]
    vq = jnp.where(valid, 1.0, 0.0) + q
    grad = grad + q * hard - vq * keys[0][...].astype(F32)
    out[...] = (SCALE * grad).astype(BF16)


def premises_kernel(size, *refs):
    keys = refs[:size]
    own, sib, lse, qval, stats, stats_sib, near = refs[size : size + 7]
    far = refs[size + 7 :]
    rows = own.shape[0]
    both = jnp.concatenate([own[...], sib[: own.shape[0], :]], axis=0)
    row_ok = valid_lanes(stats, stats_sib, 0, rows)
    held = jnp.concatenate([key[...] for key in keys], axis=0)
    scores = SCALE * dot(held, both, ((1,), (1,)))
    ok = jnp.logical_and(is_valid(held), row_ok)
    prob = jnp.where(ok, jnp.exp(scores - lse[0:1, :]), 0.0).astype(BF16)
    grad = dot(prob, both, ((1,), (0,)))
    vq = jnp.where(is_valid(keys[0]), 1.0, 0.0) + qval[...].T[:, 0:1]
    near[...] = grad[:rows] - SCALE * vq * own[...].astype(F32)
    for i, out in enumerate(far):
        out[...] = grad[(i + 1) * rows : (i + 2) * rows].astype(BF16)


def finish_kernel(size, grad_states, grad, home, meta, *refs):
    far, (out_states, out) = refs[:size], refs[size:]
    place = place_of(grad.shape[0], meta[1:2, 0 : home.shape[0]])
    summed = grad[...] + dot(place, home[...], ((1,), (0,)))
    for block in far:
        summed = summed + block[...].astype(F32)
    out[...] = summed.astype(BF16)
    out_states[...] = grad_states[...]


def loss_kernel(count, part, other, out):
    odd = jnp.full((1, 1), lax.axis_index("loop") & 1, jnp.int32) == 1
    out[...] = jnp.where(odd, part[0:1, 0:1], other[0:1, 0:1]) / count


def across_chips(held, bits):
    for bit in reversed(range(1, bits)):
        held.update({m | 1 << bit: swap(b, "loop", 1 << bit) for m, b in held.items()})
    return held


def from_sibling(held):
    for m in [m for m in held if not m & 1 and m | 1 not in held]:
        held[m | 1] = swap(held[m], "loop", 1)
    return [held[m] for m in range(len(held))]


def body(states, premises, counts, partner_mask, send_rows, hard_idx):
    rows, width = states.shape
    offer = send_rows.shape[2]
    loop_size = lax.axis_size("loop")
    group_size = lax.axis_size("groups")
    loop_bits = loop_size.bit_length() - 1
    group_bits = group_size.bit_length() - 1

    def after(value, *earlier):
        return lax.optimization_barrier((value, *earlier))[0] if earlier else value

    sources = (premises, send_rows[0], hard_idx[None, :], partner_mask[None, :], counts)
    marked = call(
        mark_kernel,
        "mark",
        shape((rows, width)),
        premises,
        counts,
        ins={0: HBM, 1: SMEM},
        scratch=[pltpu.SemaphoreType.DMA((1,))],
        vmem=40 << 20,
    )
    offered, meta = call(
        functools.partial(front_kernel, len(sources)),
        "front",
        (shape((offer, width)), shape((8, rows), jnp.int32)),
        *sources,
        ins={i: HBM for i in range(len(sources))},
        scratch=[pltpu.VMEM(source.shape, source.dtype) for source in sources]
        + [pltpu.SemaphoreType.DMA((len(sources),))],
        vmem=40 << 20,
    )
    keys = across_chips({0: marked}, loop_bits)
    both = call(
        pair_kernel, "pair", shape((2 * rows, width)), states, marked, cost=int(1.7e10)
    )
    both_sib = swap(both, "loop", 1)

    def route(m):
        return lambda block: block if m == 0 else swap(block, "groups", m)

    pool = lax.switch(partner_mask[0], [route(m) for m in range(group_size)], offered)

    even = range(0, loop_size, 2)
    forward = dict(keys)
    for m in even:
        if m:
            keys[m] = after(keys[m], pool)
    stats, qval = call(
        functools.partial(early_kernel, len(even)),
        "early",
        (shape((8, 2 * rows), F32), shape((rows, rows), F32)),
        states,
        both_sib,
        pool,
        meta,
        *(keys[m] for m in even),
    )
    stats_sib = swap(stats, "loop", 1)
    back = call(
        back_kernel, "back", shape((offer, width)), after(states, stats), qval, meta
    )
    stats_sib = after(stats_sib, back)
    lse, message = call(
        near_kernel,
        "near",
        (shape((8, 2 * rows), F32), shape((offer, width + LANES))),
        stats,
        stats_sib,
        back,
    )
    held = [keys[m] for m in even]
    for m in even[1:]:
        keys[m | 1] = swap(after(forward[m], pool), "loop", 1)
    keys[1] = both_sib
    keys = [keys[m] for m in range(loop_size)]

    def states_part():
        return call(
            functools.partial(states_kernel, loop_size),
            "states",
            shape((rows, width)),
            premises,
            *keys[1:],
            states,
            lse,
            pool,
            meta,
            qval,
            stats,
            stats_sib,
            cost=int(1.7e10),
        )

    def premises_part(lse):
        grad, *far = call(
            functools.partial(premises_kernel, len(even)),
            "premises",
            (shape((rows, width), F32),) + (shape((rows, width)),) * (len(even) - 1),
            *held,
            states,
            both_sib,
            lse,
            qval,
            stats,
            stats_sib,
            cost=int(1.7e10),
        )
        return grad, far

    def send(far):
        return [swap(block, "loop", m) for m, block in zip(even[1:], far)]

    def finish(grad_states, grad, home, sent):
        return call(
            functools.partial(finish_kernel, len(sent)),
            "finish",
            (shape((rows, width)), shape((rows, width))),
            grad_states,
            grad,
            home,
            meta,
            *sent,
        )

    def odd_core():
        held = message
        order = [*range(group_bits - 2), group_bits - 1, group_bits - 2]
        for step, level in enumerate(order):
            last = step == group_bits - 1
            if step == 0:
                grad, far = premises_part(after(lse, held))
            other = swap(held, "groups", 1 << level)
            if step == 0:
                other = after(other, grad, *far)
                sent = send(far)
            if step == 2:
                grad_states = states_part()
                other = after(other, grad_states)
            held = call(
                functools.partial(merge_kernel, level, last),
                "merge",
                (shape((offer, width)), shape((8, LANES), F32)) if last else shape(held.shape),
                held,
                other,
                meta,
            )
        home, part = held
        grads = finish(grad_states, grad, home, sent)
        for bit in range(1, loop_bits):
            other = swap(part, "loop", 1 << bit)
            part = part + (after(other, *grads) if bit == 1 else other)
        return part, *grads

    def even_core():
        grad, far = premises_part(lse)
        sent = send(far)
        home = lax.switch(
            partner_mask[0], [route(m) for m in range(group_size)], after(back, grad)
        )
        return jnp.zeros((8, LANES), F32), *finish(states_part(), grad, home, sent)

    odd = lax.axis_index("loop") & 1
    part, grad_states, grad_premises = lax.cond(odd == 1, odd_core, even_core)
    loss = call(
        functools.partial(loss_kernel, loop_size * group_size * rows),
        "loss",
        shape((1, 1), F32),
        part,
        swap(part, "loop", 1),
    )
    return loss[0, 0], grad_states, grad_premises


def solution(mesh):
    return jax.shard_map(
        body,
        mesh=mesh,
        in_specs=(
            P(("loop", "groups"), None),
            P(("loop", "groups"), None),
            P("loop", "groups"),
            P("loop"),
            P("loop", "groups", None),
            P(("loop", "groups")),
        ),
        out_specs=(P(), P(("loop", "groups"), None), P(("loop", "groups"), None)),
        check_vma=False,
    )
```

```python
import functools

import jax
import jax.numpy as jnp
from jax import lax
from jax.experimental import pallas as pl
from jax.experimental.pallas import tpu as pltpu
from jax.sharding import PartitionSpec as P

SCALE = 3.0
LANES = 128
F32 = jnp.float32
BF16 = jnp.bfloat16
VMEM = pl.BlockSpec(memory_space=pltpu.VMEM)
SMEM = pl.BlockSpec(memory_space=pltpu.SMEM)
HBM = pl.BlockSpec(memory_space=pltpu.HBM)


def swap(block, axis, mask):
    count = lax.axis_size(axis)
    return lax.ppermute(block, axis, [(i, i ^ mask) for i in range(count)])


def shape(dims, dtype=BF16):
    return jax.ShapeDtypeStruct(dims, dtype)


def call(kernel, name, outs, *args, ins=None, out_specs=None, scratch=(), cost=0, vmem=40 << 20):
    ins = ins or {}
    return pl.pallas_call(
        kernel,
        out_shape=outs,
        in_specs=[ins.get(i, VMEM) for i in range(len(args))],
        out_specs=out_specs or jax.tree.map(lambda _: VMEM, outs),
        scratch_shapes=scratch,
        compiler_params=pltpu.CompilerParams(vmem_limit_bytes=vmem),
        cost_estimate=pl.CostEstimate(flops=cost, bytes_accessed=0, transcendentals=0),
        name=name,
    )(*args)


def dot(a, b, dims):
    return lax.dot_general(a, b, (dims, ((), ())), preferred_element_type=F32)


def total(x):
    return jnp.sum(jnp.sum(x, axis=0, keepdims=True), axis=1, keepdims=True)


def parts(x):
    hi = x.astype(BF16)
    rest = x - hi.astype(F32)
    mid = rest.astype(BF16)
    low = (rest - mid.astype(F32)).astype(BF16)
    return hi, mid, low


def place_of(rows, picked):
    slot = lax.broadcasted_iota(jnp.int32, (rows, picked.shape[1]), 0)
    return jnp.where(slot == picked, 1.0, 0.0).astype(BF16)


def pick_of(offer, hard_idx):
    which = lax.broadcasted_iota(jnp.int32, (offer, hard_idx.shape[1]), 0)
    return jnp.where(which == hard_idx, 1.0, 0.0)


def column(rows):
    return lax.broadcasted_iota(jnp.int32, (rows, 1), 0).astype(F32)


def pack(message, block, scalar):
    offer, width = block.shape
    message[:, :width] = block.astype(BF16)
    row = lax.broadcasted_iota(jnp.int32, (offer, LANES), 0)
    hi, mid, low = (p.astype(F32) for p in parts(jnp.broadcast_to(scalar, row.shape)))
    spread = jnp.where(row == 0, hi, jnp.where(row == 1, mid, jnp.where(row == 2, low, 0.0)))
    message[:, width:] = spread.astype(BF16)


def unpack(message):
    width = message.shape[1] - LANES
    spread = message[:, width:].astype(F32)
    return message[:, :width], jnp.sum(spread, axis=0, keepdims=True)[:, 0:1]


def mark_kernel(premises, count, marked, sems):
    rows = premises.shape[0]
    size = rows // 1
    pieces = [pl.ds(i * size, size) for i in range(1)]
    copies = [
        pltpu.make_async_copy(premises.at[piece, :], marked.at[piece, :], sems.at[i])
        for i, piece in enumerate(pieces)
    ]
    for copy in copies:
        copy.start()
    for i, copy in enumerate(copies):
        copy.wait()
        row = lax.broadcasted_iota(jnp.int32, (size, LANES), 0) + i * size
        lane = lax.broadcasted_iota(jnp.int32, (size, LANES), 1)
        invalid = jnp.logical_and(row >= count[0, 0], lane == 0)
        first = marked[pieces[i], :LANES].astype(F32)
        marked[pieces[i], :LANES] = jnp.where(invalid, jnp.inf, first).astype(BF16)


def is_valid(key):
    return key[:, 0:1].astype(F32) < jnp.inf


def count_of(meta):
    return meta[3:4, 0:1].astype(F32)


def front_kernel(size, *refs):
    sources, (offered, meta), held = refs[:size], refs[size : size + 2], refs[size + 2 : -1]
    sems = refs[-1]
    copies = [
        pltpu.make_async_copy(source, target, sems.at[i])
        for i, (source, target) in enumerate(zip(sources, held))
    ]
    for copy in copies:
        copy.start()
    for copy in copies:
        copy.wait()
    premises, send_rows, hard_idx, mask, counts = held
    row = lax.broadcasted_iota(jnp.int32, meta.shape, 0)
    meta[...] = jnp.where(
        row == 0, hard_idx[...], jnp.where(row == 2, mask[...], counts[...])
    )
    meta[1:2, 0 : send_rows.shape[1]] = send_rows[...]
    place = place_of(premises.shape[0], send_rows[...])
    offered[...] = dot(place, premises[...], ((0,), (0,))).astype(BF16)


def back_kernel(states, qval, meta, back):
    offer = back.shape[0]
    weight = qval[:offer, :] * pick_of(offer, meta[0:1, :])
    split = jnp.concatenate(parts(weight), axis=0)
    summed = dot(split, states[...], ((1,), (0,)))
    summed = summed[:offer] + summed[offer : 2 * offer] + summed[2 * offer :]
    back[...] = (SCALE * summed).astype(BF16)


def line(width):
    return lax.broadcasted_iota(jnp.int32, (1, width), 1).astype(F32)


def mask_keys(scores, ok):
    return jnp.where(ok, scores, -jnp.inf)


def score(key, block, limit):
    return mask_keys(SCALE * dot(key, block, ((1,), (1,))), column(key.shape[0]) < limit)


def tops(blocks):
    return jnp.max(functools.reduce(jnp.maximum, blocks), axis=0, keepdims=True)


def masses(blocks, top):
    weights = functools.reduce(jnp.add, [jnp.exp(block - top) for block in blocks])
    return jnp.sum(weights, axis=0, keepdims=True)


def early_kernel(size, own, sib, pool, meta, *refs):
    keys, (stats, qval) = refs[:size], refs[size:]
    rows, offer = own.shape[0], pool.shape[0]
    both = jnp.concatenate([own[...], sib[...]], axis=0)
    oks = [is_valid(key) for key in keys]
    blocks = [SCALE * dot(key[...], both, ((1,), (1,))) for key in keys]
    slot = lax.broadcasted_iota(jnp.int32, (rows, rows), 0)
    mine = slot == lax.broadcasted_iota(jnp.int32, (rows, rows), 1)
    pos = jnp.sum(jnp.where(mine, blocks[0][:, :rows], 0.0), axis=0, keepdims=True)
    blocks = [mask_keys(block, ok) for block, ok in zip(blocks, oks)]
    top = tops(blocks)
    stats[0:1, :] = top
    stats[1:2, :] = masses(blocks, top)
    pick = pick_of(offer, meta[0:1, :])
    tval = SCALE * dot(pool[...], own[...], ((1,), (1,)))
    tval = jnp.sum(pick * tval, axis=0, keepdims=True)
    valid = line(rows) < count_of(meta)
    gap = tval - pos
    q = jnp.where(valid, 1.0 / (1.0 + jnp.exp(-gap)), 0.0)
    plus = jnp.maximum(gap, 0.0) + jnp.log(1.0 + jnp.exp(-jnp.abs(gap)))
    qval[...] = jnp.broadcast_to(q, qval.shape)
    info = jnp.broadcast_to(total(jnp.where(valid, plus - pos, 0.0)), (1, stats.shape[1]))
    for i, ok in enumerate(oks):
        info = jnp.where(line(stats.shape[1]) == 1 + i, total(jnp.where(ok, 1.0, 0.0)), info)
    stats[2:3, :] = info


def limit_of(stats, stats_sib, m):
    return (stats_sib if m & 1 else stats)[2:3, 1 + (m >> 1) : 2 + (m >> 1)]


def valid_lanes(stats, stats_sib, m, rows):
    slots = line(rows)
    pair = [slots < limit_of(stats, stats_sib, m + i) for i in range(2)]
    return jnp.concatenate(pair, axis=1)


def near_kernel(stats, stats_sib, back, lse, message):
    rows = stats.shape[1] // 2
    top, mass = stats[0:1, :], stats[1:2, :]
    flip = [
        jnp.concatenate([stats_sib[i : i + 1, rows:], stats_sib[i : i + 1, :rows]], axis=1)
        for i in range(2)
    ]
    best = jnp.maximum(top, flip[0])
    mass = mass * jnp.exp(top - best) + flip[1] * jnp.exp(flip[0] - best)
    out = best + jnp.log(mass)
    lse[...] = jnp.broadcast_to(out, lse.shape)
    out = jnp.where(valid_lanes(stats, stats_sib, 0, rows), out, 0.0)
    pack(message, back[...], total(out) + stats[2:3, 0:1] + stats_sib[2:3, 0:1])


def merge_kernel(level, last, mine, other, meta, *outs):
    block, scalar = unpack(mine)
    other_block, other_scalar = unpack(other)
    take = meta[2:3, 0:1] >> level & 1
    block = jnp.where(take == 1, other_block.astype(F32), block.astype(F32)).astype(BF16)
    scalar = scalar + other_scalar
    if last:
        outs[0][...] = block
        outs[1][...] = jnp.broadcast_to(scalar, outs[1].shape)
    else:
        pack(outs[0], block, scalar)


def states_kernel(size, *refs):
    keys = refs[:size]
    states, lse, pool, meta, qval, stats, stats_sib, out = refs[size:]
    rows, offer = states.shape[0], pool.shape[0]
    slot = column(rows)
    valid = slot < count_of(meta)
    limits = [limit_of(stats, stats_sib, m) for m in range(size)]
    cleared = [keys[0][...]] + [
        jnp.where(slot < limit, key[...].astype(F32), 0.0).astype(BF16)
        for key, limit in zip(keys[1:], limits[1:])
    ]
    cleared = jnp.concatenate(cleared, axis=0)
    scores = SCALE * dot(states[...], cleared, ((1,), (1,)))
    lse_column = jnp.broadcast_to(lse[0:1, :rows], (rows, rows)).T[:, 0:1]
    ok = jnp.concatenate([line(rows) < limit for limit in limits], axis=1)
    prob = jnp.where(jnp.logical_and(valid, ok), jnp.exp(scores - lse_column), 0.0)
    grad = dot(prob.astype(BF16), cleared, ((1,), (0,)))
    hard = dot(pick_of(offer, meta[0:1, :]).astype(BF16), pool[...], ((0,), (0,)))
    q = qval[...].T[:, 0:1]
    vq = jnp.where(valid, 1.0, 0.0) + q
    grad = grad + q * hard - vq * keys[0][...].astype(F32)
    out[...] = (SCALE * grad).astype(BF16)


def premises_kernel(size, *refs):
    keys = refs[:size]
    own, sib, lse, qval, stats, stats_sib, near = refs[size : size + 7]
    far = refs[size + 7 :]
    rows = own.shape[0]
    both = jnp.concatenate([own[...], sib[...]], axis=0)
    row_ok = valid_lanes(stats, stats_sib, 0, rows)
    held = jnp.concatenate([key[...] for key in keys], axis=0)
    scores = SCALE * dot(held, both, ((1,), (1,)))
    ok = jnp.logical_and(is_valid(held), row_ok)
    prob = jnp.where(ok, jnp.exp(scores - lse[0:1, :]), 0.0).astype(BF16)
    grad = dot(prob, both, ((1,), (0,)))
    vq = jnp.where(is_valid(keys[0]), 1.0, 0.0) + qval[...].T[:, 0:1]
    near[...] = grad[:rows] - SCALE * vq * own[...].astype(F32)
    for i, out in enumerate(far):
        out[...] = grad[(i + 1) * rows : (i + 2) * rows].astype(BF16)


def finish_kernel(size, grad_states, grad, home, meta, *refs):
    far, (out_states, out) = refs[:size], refs[size:]
    place = place_of(grad.shape[0], meta[1:2, 0 : home.shape[0]])
    summed = grad[...] + dot(place, home[...], ((1,), (0,)))
    for block in far:
        summed = summed + block[...].astype(F32)
    out[...] = summed.astype(BF16)
    out_states[...] = grad_states[...]


def loss_kernel(count, part, other, out):
    odd = jnp.full((1, 1), lax.axis_index("loop") & 1, jnp.int32) == 1
    out[...] = jnp.where(odd, part[0:1, 0:1], other[0:1, 0:1]) / count


def across_chips(held, bits):
    for bit in reversed(range(1, bits)):
        held.update({m | 1 << bit: swap(b, "loop", 1 << bit) for m, b in held.items()})
    return held


def from_sibling(held):
    for m in [m for m in held if not m & 1 and m | 1 not in held]:
        held[m | 1] = swap(held[m], "loop", 1)
    return [held[m] for m in range(len(held))]


def body(states, premises, counts, partner_mask, send_rows, hard_idx):
    rows, width = states.shape
    offer = send_rows.shape[2]
    loop_size = lax.axis_size("loop")
    group_size = lax.axis_size("groups")
    loop_bits = loop_size.bit_length() - 1
    group_bits = group_size.bit_length() - 1

    def after(value, *earlier):
        return lax.optimization_barrier((value, *earlier))[0] if earlier else value

    sources = (premises, send_rows[0], hard_idx[None, :], partner_mask[None, :], counts)
    marked = call(
        mark_kernel,
        "mark",
        shape((rows, width)),
        premises,
        counts,
        ins={0: HBM, 1: SMEM},
        scratch=[pltpu.SemaphoreType.DMA((1,))],
        vmem=40 << 20,
    )
    offered, meta = call(
        functools.partial(front_kernel, len(sources)),
        "front",
        (shape((offer, width)), shape((8, rows), jnp.int32)),
        *sources,
        ins={i: HBM for i in range(len(sources))},
        scratch=[pltpu.VMEM(source.shape, source.dtype) for source in sources]
        + [pltpu.SemaphoreType.DMA((len(sources),))],
        vmem=40 << 20,
    )
    keys = across_chips({0: marked}, loop_bits)
    states_sib = swap(states, "loop", 1)

    def route(m):
        return lambda block: block if m == 0 else swap(block, "groups", m)

    pool = lax.switch(partner_mask[0], [route(m) for m in range(group_size)], offered)

    even = range(0, loop_size, 2)
    forward = dict(keys)
    for m in even:
        if m:
            keys[m] = after(keys[m], pool)
    stats, qval = call(
        functools.partial(early_kernel, len(even)),
        "early",
        (shape((8, 2 * rows), F32), shape((rows, rows), F32)),
        states,
        states_sib,
        pool,
        meta,
        *(keys[m] for m in even),
    )
    stats_sib = swap(stats, "loop", 1)
    back = call(
        back_kernel, "back", shape((offer, width)), after(states, stats), qval, meta
    )
    stats_sib = after(stats_sib, back)
    lse, message = call(
        near_kernel,
        "near",
        (shape((8, 2 * rows), F32), shape((offer, width + LANES))),
        stats,
        stats_sib,
        back,
    )
    held = [keys[m] for m in even]
    for m in even:
        keys[m | 1] = swap(after(forward[m], pool), "loop", 1)
    keys = [keys[m] for m in range(loop_size)]

    def states_part():
        return call(
            functools.partial(states_kernel, loop_size),
            "states",
            shape((rows, width)),
            premises,
            *keys[1:],
            states,
            lse,
            pool,
            meta,
            qval,
            stats,
            stats_sib,
            cost=int(1.7e10),
        )

    def premises_part(lse):
        grad, *far = call(
            functools.partial(premises_kernel, len(even)),
            "premises",
            (shape((rows, width), F32),) + (shape((rows, width)),) * (len(even) - 1),
            *held,
            states,
            states_sib,
            lse,
            qval,
            stats,
            stats_sib,
            cost=int(1.7e10),
        )
        return grad, far

    def send(far):
        return [swap(block, "loop", m) for m, block in zip(even[1:], far)]

    def finish(grad_states, grad, home, sent):
        return call(
            functools.partial(finish_kernel, len(sent)),
            "finish",
            (shape((rows, width)), shape((rows, width))),
            grad_states,
            grad,
            home,
            meta,
            *sent,
        )

    def odd_core():
        held = message
        order = [*range(group_bits - 2), group_bits - 1, group_bits - 2]
        for step, level in enumerate(order):
            last = step == group_bits - 1
            if step == 0:
                grad, far = premises_part(after(lse, held))
            other = swap(held, "groups", 1 << level)
            if step == 0:
                other = after(other, grad, *far)
                sent = send(far)
            if step == 2:
                grad_states = states_part()
                other = after(other, grad_states)
            held = call(
                functools.partial(merge_kernel, level, last),
                "merge",
                (shape((offer, width)), shape((8, LANES), F32)) if last else shape(held.shape),
                held,
                other,
                meta,
            )
        home, part = held
        grads = finish(grad_states, grad, home, sent)
        for bit in range(1, loop_bits):
            other = swap(part, "loop", 1 << bit)
            part = part + (after(other, *grads) if bit == 1 else other)
        return part, *grads

    def even_core():
        grad, far = premises_part(lse)
        sent = send(far)
        home = lax.switch(
            partner_mask[0], [route(m) for m in range(group_size)], after(back, grad)
        )
        return jnp.zeros((8, LANES), F32), *finish(states_part(), grad, home, sent)

    odd = lax.axis_index("loop") & 1
    part, grad_states, grad_premises = lax.cond(odd == 1, odd_core, even_core)
    loss = call(
        functools.partial(loss_kernel, loop_size * group_size * rows),
        "loss",
        shape((1, 1), F32),
        part,
        swap(part, "loop", 1),
    )
    return loss[0, 0], grad_states, grad_premises


def solution(mesh):
    return jax.shard_map(
        body,
        mesh=mesh,
        in_specs=(
            P(("loop", "groups"), None),
            P(("loop", "groups"), None),
            P("loop", "groups"),
            P("loop"),
            P("loop", "groups", None),
            P(("loop", "groups")),
        ),
        out_specs=(P(), P(("loop", "groups"), None), P(("loop", "groups"), None)),
        check_vma=False,
    )
```
